256 devices in a mesh: lev: 4 (over z_hi), lat: 64 (over y, x, z_lo, core).
Axes of the slice: x: 4, y: 4, z: 8 (z_hi: 4, z_lo: 2; z = z_hi * 2 + z_lo), core: 2. Of those that a mesh axis runs over, the one named last changes fastest.
Arguments:
- field: bfloat16 [12, 256, 360, 128], P('lev', 'lat'), may hold values from -6 to 6
- level_count: int32 [4], replicated, may hold values from 1 to 3, as said below
- tap_rows: int32 [256, 8], replicated, may hold values from -2 to 2
- tap_lons: int32 [256, 8], replicated, may hold values from -4 to 4
- tap_values: float32 [256, 8, 4], replicated, may hold values from -2.1 to 2.1
- norm_gain: float32 [2, 128], replicated, may hold values from 0.5 to 1.5
- disco_weight: bfloat16 [2, 512, 128], replicated, may hold values from -0.25 to 0.25
- vert_weight: bfloat16 [2, 384, 128], replicated, may hold values from -0.3125 to 0.3125
Outputs:
- result: bfloat16 [12, 256, 360, 128], P('lev', 'lat')
The draws below stay inside these ranges and needn't reach their ends.
Inputs may be any that keep to these rules, and one draw needn't show every extreme that they name: Group g holds the next level_count[g] levels from the lowest up; the entries sum to 9 and the largest equals 3.
All inputs are finite; a program needn't handle non-finite values.
Results may differ from the reference program's by a relative error of at most 0.008.
Values may be sent and summed in bfloat16 or wider, within the bound.
No kernel may reach another device: no remote copies, remote signals or barrier semaphores. Data moves between devices by JAX's collectives and lax.ppermute only.
A program may use at most 64 MiB of HBM per device.

```python
import jax
import jax.numpy as jnp
from jax import lax

C = 128
K = 4
TAPS = 8
H = 2
WLON = 4
LEV_CAP = 3
PASSES = 2
LON = 360
SLOTS = 12
ROWS = 256
N_LEV = 4


def draw_level_count(key, part):
    key = jax.random.fold_in(key, 11)
    order_key, flip_key = jax.random.split(key)
    order = jax.random.permutation(order_key, N_LEV)
    flip = jax.random.randint(flip_key, (), 0, 2).astype(jnp.int32)
    group_ids = jnp.arange(N_LEV, dtype=jnp.int32)
    first = (group_ids == order[0]).astype(jnp.int32)
    giver = (group_ids == order[1]).astype(jnp.int32)
    taker = (group_ids == order[2]).astype(jnp.int32)
    return (2 + first + flip * (taker - giver)).astype(jnp.int32)


def with_ends(result, rng, least, high):
    longest = result.shape.index(max(result.shape))
    spots = []
    for shift in (0, 1):
        where = [jax.random.randint(jax.random.fold_in(rng, axis), (), 0, length) for axis, length in enumerate(result.shape)]
        where[longest] = (where[longest] + shift) % result.shape[longest]
        spots.append(tuple(where))
    return result.at[spots[0]].set(least).at[spots[1]].set(high)


def block_scale(rng, shape, shards, low, high):
    level, own = 1.0, jax.random.fold_in(rng, 6)
    for dim, parts in shards:
        draws = jnp.exp(jax.random.uniform(jax.random.fold_in(own, dim), (parts,), jnp.float32, low / len(shards), high / len(shards)))
        level = level * jnp.repeat(draws, shape[dim] // parts).reshape([-1 if axis == dim else 1 for axis in range(len(shape))])
    return level


def gaussian(key, extent, spread, reach, cuts=(), kind=jnp.bfloat16):
    level = block_scale(key, extent, cuts, -0.22, 0.18) if cuts else 1.0
    entries = jax.random.normal(key, extent, jnp.float32) * spread * level
    return jnp.minimum(jnp.maximum(entries, -reach), reach).astype(kind)


def setup_inputs(seed: int = 0) -> dict:
    keys = jax.random.split(jax.random.key(seed), 9)
    return {
        "field": gaussian(keys[0], (SLOTS, ROWS, LON, C), 1.0, 6.0, ((0, 4), (1, 64))),
        "level_count": draw_level_count(jax.random.fold_in(keys[8], 71), 0),
        "tap_rows": with_ends(jax.random.randint(keys[2], (ROWS, TAPS), -H, H + 1), jax.random.fold_in(keys[2], 1), -H, H).astype(jnp.int32),
        "tap_lons": with_ends(jax.random.randint(keys[3], (ROWS, TAPS), -WLON, WLON + 1), jax.random.fold_in(keys[3], 1), -WLON, WLON).astype(jnp.int32),
        "tap_values": gaussian(keys[4], (ROWS, TAPS, K), 0.35, 2.1, (), jnp.float32),
        "norm_gain": jnp.clip(jax.random.uniform(keys[5], (PASSES, C), jnp.float32, 0.5, 1.5), 0.5, 1.5),
        "disco_weight": gaussian(keys[6], (PASSES, K * C, C), (K * C) ** -0.5, 0.25),
        "vert_weight": gaussian(keys[7], (PASSES, 3 * C, C), (3 * C) ** -0.5, 0.3125),
    }


EPSILON = 1e-06

def normalize(values, gain):
    widened = values.astype(jnp.float32)
    mean_square = lax.optimization_barrier(jnp.mean(widened * widened, axis=-1, keepdims=True))
    return (widened * lax.rsqrt(mean_square + EPSILON) * gain).astype(jnp.bfloat16)

def filter_plane(padded, row_table, lon_table, value_table, weight):
    row_count = row_table.shape[0]
    lon_count = padded.shape[1]
    channels = padded.shape[2]
    flat_plane = padded.reshape(padded.shape[0] * lon_count, channels)
    row_ids = jnp.arange(row_count, dtype=jnp.int32)[:, None]
    lon_ids = jnp.arange(lon_count, dtype=jnp.int32)[None, :]
    total = jnp.zeros((row_count, lon_count, K, channels), jnp.float32)
    for tap_index in range(TAPS):
        source_rows = row_ids + row_table[:, tap_index:tap_index + 1] + H
        source_lons = (lon_ids + lon_table[:, tap_index:tap_index + 1]) % lon_count
        picked = jnp.take(flat_plane, source_rows * lon_count + source_lons, axis=0).astype(jnp.float32)
        total = total + value_table[:, tap_index, :][:, None, :, None] * picked[:, :, None, :]
    filtered = total.astype(jnp.bfloat16).reshape(row_count * lon_count, K * channels)
    mixed = jnp.dot(filtered, weight, preferred_element_type=jnp.float32)
    return mixed.astype(jnp.bfloat16).reshape(row_count, lon_count, channels)

def reference(field, level_count, tap_rows, tap_lons, tap_values, norm_gain, disco_weight, vert_weight):
    groups = level_count.shape[0]
    slot_total = groups * LEV_CAP
    slot_ids = jnp.arange(slot_total, dtype=jnp.int32)
    group_ids = slot_ids // LEV_CAP
    inner_ids = slot_ids % LEV_CAP
    own_count = level_count[group_ids]
    alive = inner_ids < own_count
    lower_group = jnp.maximum(group_ids - 1, 0)
    upper_group = jnp.minimum(group_ids + 1, groups - 1)
    below_index = jnp.where(inner_ids > 0, slot_ids - 1, lower_group * LEV_CAP + level_count[lower_group] - 1)
    below_valid = (inner_ids > 0) | (group_ids > 0)
    above_index = jnp.where(inner_ids + 1 < own_count, slot_ids + 1, upper_group * LEV_CAP)
    above_valid = (inner_ids + 1 < own_count) | (group_ids < groups - 1)
    current = field
    for pass_index in range(PASSES):
        normed = normalize(current, norm_gain[pass_index])
        padded = jnp.pad(normed, ((0, 0), (H, H), (0, 0), (0, 0)))
        disco_map = disco_weight[pass_index]

        def filter_slot(plane, disco_map=disco_map):
            return filter_plane(plane, tap_rows, tap_lons, tap_values, disco_map)
        disco = lax.map(filter_slot, padded)
        vertical_weight = vert_weight[pass_index]

        def mix_slot(items, disco=disco, vertical_weight=vertical_weight):
            below_at, above_at, below_ok, above_ok, slot_alive, residual, plane = items
            below = jnp.where(below_ok, disco[below_at], jnp.zeros_like(plane))
            above = jnp.where(above_ok, disco[above_at], jnp.zeros_like(plane))
            stacked = jnp.concatenate([below, plane, above], axis=-1)
            vertical = jnp.dot(stacked.reshape(-1, 3 * C), vertical_weight, preferred_element_type=jnp.float32)
            vertical = vertical.reshape(plane.shape)
            updated = residual.astype(jnp.float32) + jax.nn.gelu(vertical, approximate=False)
            return jnp.where(slot_alive, updated, jnp.zeros_like(updated)).astype(jnp.bfloat16)
        current = lax.map(mix_slot, (below_index, above_index, below_valid, above_valid, alive, current, disco))
    return current
```

```python
import jax
import jax.numpy as jnp
from jax import lax
from jax.experimental import pallas as pl
from jax.experimental.pallas import tpu as pltpu
from jax.sharding import PartitionSpec as P

K = 4
TAPS = 8
H = 2
PASSES = 2
PAD = 8
EPSILON = 1e-06

BF16 = jnp.bfloat16
F32 = jnp.float32
VMEM = pl.BlockSpec(memory_space=pltpu.VMEM)
SMEM = pl.BlockSpec(memory_space=pltpu.SMEM)
LIMIT = 24 * 1024 * 1024


def call(kernel, out_shape, in_specs, scratch=(), flops=0, nbytes=0):
    many = isinstance(out_shape, (tuple, list))
    return pl.pallas_call(
        kernel,
        out_shape=out_shape,
        in_specs=in_specs,
        out_specs=[VMEM] * len(out_shape) if many else VMEM,
        scratch_shapes=list(scratch),
        compiler_params=pltpu.CompilerParams(vmem_limit_bytes=LIMIT),
        cost_estimate=pl.CostEstimate(flops=flops, bytes_accessed=nbytes, transcendentals=0),
    )


def normed(widened, gain):
    mean_square = jnp.mean(widened * widened, axis=-1, keepdims=True)
    return widened * lax.rsqrt(mean_square + EPSILON) * gain


def norm_kernel(field, gain, head, tail):
    slots, rows = field.shape[:2]
    for slot in range(slots):
        for row in range(rows):
            value = normed(field[slot, row].astype(F32), gain[0:1, :]).astype(BF16)
            if row < H:
                head[slot, row] = value
            else:
                tail[slot, row - H] = value


def tap_map_kernel(values, weight, *outs):
    channels = weight.shape[-1]
    rows = values.shape[0]
    for p in range(PASSES):

        def one(index, carry, p=p):
            row = index // TAPS
            tap = index % TAPS
            total = None
            for k in range(K):
                part = values[row, tap * K + k] * weight[p, k * channels : (k + 1) * channels, :].astype(F32)
                total = part if total is None else total + part
            outs[p][row, pl.ds(pl.multiple_of(tap * channels, channels), channels), :] = total.astype(BF16)
            return carry

        lax.fori_loop(0, rows * TAPS, one, 0)


def stage(scratch, place, slot, head, tail, low, high):
    lons = head.shape[2]
    for row, (ref, at) in enumerate(
        [(low, 0), (low, 1), (head, 0), (head, 1), (tail, 0), (tail, 1), (high, 0), (high, 1)]
    ):
        value = ref[slot, at].astype(F32)
        scratch[place, row, pl.ds(PAD, lons), :] = value
        scratch[place, row, pl.ds(0, PAD), :] = value[lons - PAD :]
        scratch[place, row, pl.ds(PAD + lons, PAD), :] = value[:PAD]


def disco_rows(scratch, place, row_table, lon_table, weights, out):
    rows, lons = out.shape[0], out.shape[1]

    def one(row, carry):
        parts = []
        for tap in range(TAPS):
            source = row + row_table[row, tap] + H
            start = lon_table[row, tap] + PAD
            parts.append(scratch[place, source, pl.ds(start, lons), :].astype(BF16))
        lhs = jnp.concatenate(parts, axis=1)
        total = jnp.dot(lhs, weights[row], preferred_element_type=F32)
        out[row] = total.astype(BF16)
        return carry

    lax.fori_loop(0, rows, one, 0)


def ends_kernel(count, row_table, lon_table, head, tail, low, high, weights, bottom, top, scratch):
    last = count[0] - 1
    stage(scratch, 0, 0, head, tail, low, high)
    stage(scratch, 1, last, head, tail, low, high)
    disco_rows(scratch, 0, row_table, lon_table, weights, bottom)
    disco_rows(scratch, 1, row_table, lon_table, weights, top)


def middle_kernel(row_table, lon_table, head, tail, low, high, weights, middle, scratch):
    stage(scratch, 0, 1, head, tail, low, high)
    disco_rows(scratch, 0, row_table, lon_table, weights, middle)


def erf(x):
    return lax.erf(x)


def gelu(v):
    return 0.5 * v * (1.0 + erf(v * 0.7071067811865476))


def mix(below, disco, above, weight):
    stacked = jnp.concatenate([below, disco, above], axis=1)
    return gelu(jnp.dot(stacked, weight[...], preferred_element_type=F32))


def mix_rows(count, current, bottom, middle, top, from_below, from_above, weight, put):
    rows = current.shape[1]
    own = count[0]

    def one(row, carry):
        b, m, t = bottom[row], middle[row], top[row]
        lo, hi = from_below[row], from_above[row]
        three, two, single = own == 3, own == 2, own == 1
        first = mix(lo, b, jnp.where(single, hi, jnp.where(two, t, m)), weight)
        last = mix(jnp.where(single, lo, jnp.where(two, b, m)), t, hi, weight)
        inner = mix(b, m, t, weight)
        x0 = current[0, row].astype(F32) + first
        x1 = current[1, row].astype(F32) + jnp.where(three, inner, last)
        x2 = current[2, row].astype(F32) + last
        put(0, row, x0.astype(BF16))
        put(1, row, jnp.where(own >= 2, x1, 0.0).astype(BF16))
        put(2, row, jnp.where(three, x2, 0.0).astype(BF16))
        return carry

    lax.fori_loop(0, rows, one, 0)


def inner_mix_kernel(count, current, bottom, middle, top, from_below, from_above, weight, gain, out, head, tail):
    rows = current.shape[1]

    def put(slot, row, value):
        out[slot, row] = value

    mix_rows(count, current, bottom, middle, top, from_below, from_above, weight, put)
    for slot in range(current.shape[0]):
        for row in range(rows):
            value = normed(out[slot, row].astype(F32), gain[0:1, :]).astype(BF16)
            if row < H:
                head[slot, row] = value
            else:
                tail[slot, row - H] = value


def last_mix_kernel(count, current, bottom, middle, top, from_below, from_above, weight, out):
    def put(slot, row, value):
        out[slot, row] = value

    mix_rows(count, current, bottom, middle, top, from_below, from_above, weight, put)


def on_device(field, level_count, tap_rows, tap_lons, tap_values, norm_gain, disco_weight, vert_weight):
    slots, rows, lons, channels = field.shape
    first_row = lax.axis_index("lat") * rows
    count = lax.dynamic_slice_in_dim(level_count, lax.axis_index("lev"), 1, 0)
    row_part = lax.dynamic_slice_in_dim(tap_rows, first_row, rows, 0)
    lon_part = lax.dynamic_slice_in_dim(tap_lons, first_row, rows, 0)
    value_part = lax.dynamic_slice_in_dim(tap_values, first_row, rows, 0).reshape(rows, TAPS * K)
    lats = lax.axis_size("lat")
    levs = lax.axis_size("lev")
    up = [(i, i + 1) for i in range(lats - 1)]
    down = [(i + 1, i) for i in range(lats - 1)]
    level_up = [(i, i + 1) for i in range(levs - 1)]
    level_down = [(i + 1, i) for i in range(levs - 1)]

    edge = jax.ShapeDtypeStruct((slots, H, lons, channels), BF16)
    plane = jax.ShapeDtypeStruct((rows, lons, channels), BF16)
    whole = jax.ShapeDtypeStruct(field.shape, BF16)
    padded = lons + 2 * PAD

    head, tail = call(norm_kernel, [edge, edge], [VMEM, VMEM], nbytes=2 * field.size * 2)(field, norm_gain[0:1])
    maps = call(
        tap_map_kernel,
        [jax.ShapeDtypeStruct((rows, TAPS * channels, channels), BF16)] * PASSES,
        [SMEM, VMEM],
        flops=8 * PASSES * rows * TAPS * channels * channels,
        nbytes=1 << 21,
    )(value_part, disco_weight)
    current = field
    for p in range(PASSES):
        low = lax.ppermute(tail, "lat", up)
        high = lax.ppermute(head, "lat", down)
        dots = 2 * rows * lons * TAPS * channels * channels
        bottom, top = call(
            ends_kernel,
            [plane, plane],
            [SMEM, SMEM, SMEM, VMEM, VMEM, VMEM, VMEM, VMEM],
            [pltpu.VMEM((2, rows + 2 * H, padded, channels), F32)],
            flops=2 * dots,
            nbytes=1 << 22,
        )(count, row_part, lon_part, head, tail, low, high, maps[p])
        from_below = lax.ppermute(top, "lev", level_up)
        from_above = lax.ppermute(bottom, "lev", level_down)
        middle = call(
            middle_kernel,
            plane,
            [SMEM, SMEM, VMEM, VMEM, VMEM, VMEM, VMEM],
            [pltpu.VMEM((1, rows + 2 * H, padded, channels), F32)],
            flops=dots,
            nbytes=1 << 22,
        )(row_part, lon_part, head, tail, low, high, maps[p])
        operands = (count, current, bottom, middle, top, from_below, from_above, vert_weight[p])
        specs = [SMEM] + [VMEM] * 7
        if p + 1 < PASSES:
            current, head, tail = call(inner_mix_kernel, [whole, edge, edge], specs + [VMEM], flops=dots, nbytes=1 << 22)(
                *operands, norm_gain[p + 1 : p + 2]
            )
        else:
            current = call(last_mix_kernel, whole, specs, flops=dots, nbytes=1 << 22)(*operands)
    return current


def solution(mesh):
    return jax.shard_map(
        on_device,
        mesh=mesh,
        in_specs=(P("lev", "lat", None, None), P(), P(), P(), P(), P(), P(), P()),
        out_specs=P("lev", "lat", None, None),
        check_vma=False,
    )
```

```python
import functools

import jax
import jax.numpy as jnp
from jax import lax
from jax.experimental import pallas as pl
from jax.experimental.pallas import tpu as pltpu
from jax.sharding import PartitionSpec as P

K = 4
TAPS = 8
H = 2
PASSES = 2
PAD = 8
EPSILON = 1e-06

BF16 = jnp.bfloat16
F32 = jnp.float32
VMEM = pl.BlockSpec(memory_space=pltpu.VMEM)
SMEM = pl.BlockSpec(memory_space=pltpu.SMEM)
LIMIT = 24 * 1024 * 1024


def call(kernel, out_shape, in_specs, scratch=(), flops=0, nbytes=0, after=()):
    many = isinstance(out_shape, (tuple, list))
    count, late = len(in_specs), len(after)

    def body(*refs):
        kernel(*refs[:count], *refs[count + late :])

    made = pl.pallas_call(
        body,
        out_shape=out_shape,
        in_specs=list(in_specs) + [pl.BlockSpec(memory_space=pl.ANY)] * late,
        out_specs=[VMEM] * len(out_shape) if many else VMEM,
        scratch_shapes=list(scratch),
        compiler_params=pltpu.CompilerParams(vmem_limit_bytes=LIMIT),
        cost_estimate=pl.CostEstimate(flops=flops, bytes_accessed=nbytes, transcendentals=0),
    )
    return lambda *operands: made(*operands, *after)


def here(level_count):
    group = lax.axis_index("lev")
    own = level_count[group]
    return own, group % 2 == 1, lax.axis_index("lat") % 2


def plane_slots(own, group_odd):
    return jnp.where(group_odd, 0, own - 1), jnp.where(group_odd, own - 1, 0), 1


def far_row(lat_odd):
    return H * lat_odd


def near_row(lat_odd):
    return H * (1 - lat_odd)


def normed(widened, gain):
    mean_square = jnp.mean(widened * widened, axis=-1, keepdims=True)
    return (widened * lax.rsqrt(mean_square + EPSILON) * gain).astype(BF16)


def norm_kernel(level_count, field, gain, far, near):
    own, group_odd, lat_odd = here(level_count)
    for plane, slot in enumerate(plane_slots(own, group_odd)):
        for h in range(H):
            far[plane, h] = normed(field[slot, far_row(lat_odd) + h].astype(F32), gain[0:1, :])
            near[plane, h] = normed(field[slot, near_row(lat_odd) + h].astype(F32), gain[0:1, :])


def tap_map_kernel(values, weight, out):
    channels = weight.shape[-1]
    rows = values.shape[0]

    def one(index, carry):
        row = index // TAPS
        tap = index % TAPS
        total = None
        for k in range(K):
            part = values[row, tap * K + k] * weight[k * channels : (k + 1) * channels, :].astype(F32)
            total = part if total is None else total + part
        out[row, pl.ds(pl.multiple_of(tap * channels, channels), channels), :] = total.astype(BF16)
        return carry

    lax.fori_loop(0, rows * TAPS, one, 0)


def stage(scratch, place, refs, plane, firsts):
    for ref, first in zip(refs, firsts):
        lons = ref.shape[2]
        for h in range(H):
            value = ref[plane, h].astype(F32)
            scratch[place, first + h, pl.ds(PAD, lons), :] = value
            scratch[place, first + h, pl.ds(0, PAD), :] = value[lons - PAD :]
            scratch[place, first + h, pl.ds(PAD + lons, PAD), :] = value[:PAD]


def disco_kernel(planes, is_far, row_table, lon_table, far, near, got, weights, *rest):
    outs, scratch = rest[:-1], rest[-1]
    lat_odd = lax.axis_index("lat") % 2
    lons = far.shape[2]
    first = far_row(lat_odd) if is_far else near_row(lat_odd)
    got_first = 3 * H * lat_odd if is_far else 3 * H * (1 - lat_odd)
    for place, plane in enumerate(planes):
        stage(scratch, place, (far, near, got), plane, (H + far_row(lat_odd), H + near_row(lat_odd), got_first))

    def one(h, carry):
        row = first + h
        taps = [(row + row_table[row, tap] + H, lon_table[row, tap] + PAD) for tap in range(TAPS)]
        for place, out in enumerate(outs):
            parts = [scratch[place, source, pl.ds(start, lons), :].astype(BF16) for source, start in taps]
            total = jnp.dot(jnp.concatenate(parts, axis=1), weights[row], preferred_element_type=F32)
            out[h] = total.astype(BF16)
        return carry

    lax.fori_loop(0, H, one, 0)


def gelu(v):
    return 0.5 * v * (1.0 + lax.erf(v * 0.7071067811865476))


def mix(below, disco, above, weight):
    stacked = jnp.concatenate([below, disco, above], axis=1)
    return gelu(jnp.dot(stacked, weight[...], preferred_element_type=F32))


def mixed(h, own, group_odd, one, two, middle, got_one, got_two, weight):
    a, b, m = one[h], two[h], middle[h]
    for_one, for_two = got_one[h], got_two[h]
    three, single = own == 3, own == 1
    bottom, top = jnp.where(group_odd, a, b), jnp.where(group_odd, b, a)
    below, above = jnp.where(group_odd, for_one, for_two), jnp.where(group_odd, for_two, for_one)
    low = mix(below, bottom, jnp.where(single, above, jnp.where(three, m, top)), weight)
    high = mix(jnp.where(single, below, jnp.where(three, m, bottom)), top, above, weight)
    return low, high, mix(bottom, m, top, weight)


def mix_kernel(is_far, level_count, current, one, two, middle, got_one, got_two, weight, gain, new, edge):
    own, group_odd, lat_odd = here(level_count)
    first = far_row(lat_odd) if is_far else near_row(lat_odd)
    slots = (0, own - 1, 1)

    def each(h, carry):
        values = mixed(h, own, group_odd, one, two, middle, got_one, got_two, weight)
        for plane, value in enumerate(values):
            x = (current[slots[plane], first + h].astype(F32) + value).astype(BF16)
            new[plane, h] = x
            place = jnp.where(group_odd, plane, 1 - plane) if plane < 2 else plane
            edge[place, h] = normed(x.astype(F32), gain[0:1, :])
        return carry

    lax.fori_loop(0, H, each, 0)


def last_kernel(level_count, current, one, two, middle, got_one, got_two, weight, out):
    own, group_odd, _ = here(level_count)

    def each(h, carry):
        values = mixed(h, own, group_odd, one, two, middle, got_one, got_two, weight)
        bottom, top, m = [(current[p, h].astype(F32) + value).astype(BF16) for p, value in enumerate(values)]
        zero = jnp.zeros_like(top)
        out[0, h] = bottom
        out[1, h] = jnp.where(own == 3, m, jnp.where(own == 2, top, zero))
        out[2, h] = jnp.where(own == 3, top, zero)
        return carry

    lax.fori_loop(0, H, each, 0)


def final_kernel(level_count, current, one, two, middle, got_one, got_two, weight, near_rows, out):
    own, group_odd, lat_odd = here(level_count)
    for slot in range(out.shape[0]):
        for h in range(H):
            out[slot, near_row(lat_odd) + h] = near_rows[slot, h]

    def each(h, carry):
        row = far_row(lat_odd) + h
        values = mixed(h, own, group_odd, one, two, middle, got_one, got_two, weight)
        bottom, top, m = [(current[p, h].astype(F32) + value).astype(BF16) for p, value in enumerate(values)]
        zero = jnp.zeros_like(top)
        out[0, row] = bottom
        out[1, row] = jnp.where(own == 3, m, jnp.where(own == 2, top, zero))
        out[2, row] = jnp.where(own == 3, top, zero)
        return carry

    lax.fori_loop(0, H, each, 0)


def pairs(count, first):
    found = [(i, i + 1) for i in range(first, count - 1, 2)]
    return found + [(j, i) for i, j in found]


def on_device(field, level_count, tap_rows, tap_lons, tap_values, norm_gain, disco_weight, vert_weight):
    slots, rows, lons, channels = field.shape
    lats, levs = lax.axis_size("lat"), lax.axis_size("lev")
    near_pairs, far_pairs = pairs(lats, 0), pairs(lats, 1)
    one_pairs, two_pairs = pairs(levs, 0), pairs(levs, 1)
    edge = jax.ShapeDtypeStruct((slots, H, lons, channels), BF16)
    plane = jax.ShapeDtypeStruct((H, lons, channels), BF16)
    work = 12 * H * lons * TAPS * channels * channels

    first_row = lax.axis_index("lat") * rows
    row_part = lax.dynamic_slice_in_dim(tap_rows, first_row, rows, 0)
    lon_part = lax.dynamic_slice_in_dim(tap_lons, first_row, rows, 0)
    value_part = lax.dynamic_slice_in_dim(tap_values, first_row, rows, 0).reshape(rows, TAPS * K)

    def maps_of(p, after=()):
        shape = jax.ShapeDtypeStruct((rows, TAPS * channels, channels), BF16)
        return call(tap_map_kernel, shape, [SMEM, VMEM], flops=work, after=after)(value_part, disco_weight[p])

    def disco(planes, is_far, far, near, got, maps, after):
        scratch = pltpu.VMEM((len(planes), rows + 2 * H, lons + 2 * PAD, channels), F32)
        return call(
            functools.partial(disco_kernel, planes, is_far),
            [plane] * len(planes),
            [SMEM] * 2 + [VMEM] * 4,
            [scratch],
            flops=work * len(planes),
            nbytes=1 << 20,
            after=after,
        )(row_part, lon_part, far, near, got, maps)

    far, near = call(norm_kernel, [edge, edge], [SMEM, VMEM, VMEM], nbytes=1 << 21)(level_count, field, norm_gain[0:1])
    maps = maps_of(0)
    for p in range(PASSES):
        far_got = lax.ppermute(far, "lat", far_pairs)
        near_got = lax.ppermute(near, "lat", near_pairs)
        ends, after = [], []
        for is_far, got in ((False, near_got), (True, far_got)):
            one, two = disco((0, 1), is_far, far, near, got, maps, after)
            got_one = lax.ppermute(one, "lev", one_pairs)
            got_two = lax.ppermute(two, "lev", two_pairs)
            (middle,) = disco((2,), is_far, far, near, got, maps, [one])
            after = [middle]
            ends.append((one, two, middle, got_one, got_two, vert_weight[p]))
        if p + 1 < PASSES:
            maps = maps_of(p + 1, after)
            after = [maps]
            made = []
            for is_far in (False, True):
                new, edges = call(
                    functools.partial(mix_kernel, is_far),
                    [edge, edge],
                    [SMEM] + [VMEM] * 8,
                    flops=work * 2,
                    nbytes=1 << 20,
                    after=after,
                )(level_count, field, *ends[is_far], norm_gain[p + 1 : p + 2])
                made.append((new, edges))
                after = [new]
            (near_new, near), (far_new, far) = made
        else:
            near_rows = call(last_kernel, edge, [SMEM] + [VMEM] * 7, flops=work * 2, nbytes=1 << 20, after=after)(
                level_count, near_new, *ends[0]
            )
            return call(
                final_kernel, jax.ShapeDtypeStruct(field.shape, BF16), [SMEM] + [VMEM] * 8, flops=work * 2, nbytes=1 << 20
            )(level_count, far_new, *ends[1], near_rows)


def solution(mesh):
    return jax.shard_map(
        on_device,
        mesh=mesh,
        in_specs=(P("lev", "lat", None, None), P(), P(), P(), P(), P(), P(), P()),
        out_specs=P("lev", "lat", None, None),
        check_vma=False,
    )
```

```python
import functools

import jax
import jax.numpy as jnp
from jax import lax
from jax.experimental import pallas as pl
from jax.experimental.pallas import tpu as pltpu
from jax.sharding import PartitionSpec as P

K = 4
TAPS = 8
H = 2
PASSES = 2
PAD = 8
EPSILON = 1e-06

BF16 = jnp.bfloat16
F32 = jnp.float32
VMEM = pl.BlockSpec(memory_space=pltpu.VMEM)
SMEM = pl.BlockSpec(memory_space=pltpu.SMEM)
LIMIT = 24 * 1024 * 1024


def call(kernel, out_shape, in_specs, scratch=(), after=(), cost=1, out_specs=None):
    many = isinstance(out_shape, (tuple, list))
    count, late = len(in_specs), len(after)

    def body(*refs):
        kernel(*refs[:count], *refs[count + late :])

    made = pl.pallas_call(
        body,
        out_shape=out_shape,
        in_specs=list(in_specs) + [pl.BlockSpec(memory_space=pl.ANY)] * late,
        out_specs=out_specs or ([VMEM] * len(out_shape) if many else VMEM),
        scratch_shapes=list(scratch),
        compiler_params=pltpu.CompilerParams(vmem_limit_bytes=LIMIT),
        cost_estimate=pl.CostEstimate(flops=cost, bytes_accessed=1, transcendentals=0),
    )
    return lambda *operands: made(*operands, *after)


def here(level_count):
    group = lax.axis_index("lev")
    own = level_count[group]
    return own, group % 2 == 1, lax.axis_index("lat") % 2


def plane_slots(own, group_odd):
    return jnp.where(group_odd, 0, own - 1), jnp.where(group_odd, own - 1, 0), 1


def far_row(lat_odd):
    return H * lat_odd


def near_row(lat_odd):
    return H * (1 - lat_odd)


def normed(widened, gain):
    mean_square = jnp.mean(widened * widened, axis=-1, keepdims=True)
    return (widened * lax.rsqrt(mean_square + EPSILON) * gain).astype(BF16)


def norm_kernel(is_far, field, gain, out, rows, sems):
    lat_odd = lax.axis_index("lat") % 2
    first = far_row(lat_odd) if is_far else near_row(lat_odd)
    slots = out.shape[0]
    copies = [pltpu.make_async_copy(field.at[slot, pl.ds(first, H)], rows.at[slot], sems.at[slot]) for slot in range(slots)]
    for copy in copies:
        copy.start()
    for slot, copy in enumerate(copies):
        copy.wait()
        for h in range(H):
            out[slot, h] = normed(rows[slot, h].astype(F32), gain[0:1, :])


def tap_map_kernel(values, weight, out):
    channels = weight.shape[-1]
    rows = values.shape[0]

    def one(index, carry):
        row = index // TAPS
        tap = index % TAPS
        total = None
        for k in range(K):
            part = values[row, tap * K + k] * weight[k * channels : (k + 1) * channels, :].astype(F32)
            total = part if total is None else total + part
        out[row, pl.ds(pl.multiple_of(tap * channels, channels), channels), :] = total.astype(BF16)
        return carry

    lax.fori_loop(0, rows * TAPS, one, 0)


def stage(scratch, place, refs, planes, firsts):
    for ref, plane, first in zip(refs, planes, firsts):
        lons = ref.shape[2]
        for h in range(H):
            value = ref[plane, h].astype(F32)
            scratch[place, first + h, pl.ds(PAD, lons), :] = value
            scratch[place, first + h, pl.ds(0, PAD), :] = value[lons - PAD :]
            scratch[place, first + h, pl.ds(PAD + lons, PAD), :] = value[:PAD]


def disco_rows(scratch, places, row, row_table, lon_table, weights, lons):
    taps = [(row + row_table[row, tap] + H, lon_table[row, tap] + PAD) for tap in range(TAPS)]
    for place in places:
        parts = [scratch[place, source, pl.ds(start, lons), :].astype(BF16) for source, start in taps]
        total = jnp.dot(jnp.concatenate(parts, axis=1), weights[row], preferred_element_type=F32)
        yield total.astype(BF16)


def places_of(level_count, is_far):
    own, group_odd, lat_odd = here(level_count)
    beyond = 3 * H * lat_odd if is_far else 3 * H * (1 - lat_odd)
    first = far_row(lat_odd) if is_far else near_row(lat_odd)
    return own, group_odd, first, (H + far_row(lat_odd), H + near_row(lat_odd), beyond)


def ends_kernel(is_far, slotted, level_count, row_table, lon_table, far, near, got, weights, one, two, scratch):
    own, group_odd, first, at = places_of(level_count, is_far)
    for place, slot in enumerate(plane_slots(own, group_odd)[:2]):
        plane = slot if slotted else place
        stage(scratch, place, (far, near, got), (plane,) * 3, at)

    def each(h, carry):
        one[h], two[h] = disco_rows(scratch, (0, 1), first + h, row_table, lon_table, weights, far.shape[2])
        return carry

    lax.fori_loop(0, H, each, 0)


def middle_kernel(is_far, planes, level_count, row_table, lon_table, far, near, got, weights, one, two, current, mixing, gain, *rest):
    middle, new, scratch = rest[0], rest[1], rest[-1]
    _, group_odd, first, at = places_of(level_count, is_far)
    stage(scratch, 0, (far, near, got), planes, at)

    def each(h, carry):
        (m,) = disco_rows(scratch, (0,), first + h, row_table, lon_table, weights, far.shape[2])
        middle[h] = m
        below, above = jnp.where(group_odd, one[h], two[h]), jnp.where(group_odd, two[h], one[h])
        old = current[1, first + h] if len(current.shape) == 4 else current[h]
        x = (old.astype(F32) + mix(below, m, above, mixing[...])).astype(BF16)
        new[h] = x
        if len(rest) == 4:
            rest[2][0, h] = normed(x.astype(F32), gain[1:2, :])
        return carry

    lax.fori_loop(0, H, each, 0)


def gelu(v):
    return 0.5 * v * (1.0 + lax.erf(v * 0.7071067811865476))


def mix(below, disco, above, weight):
    stacked = jnp.concatenate([below, disco, above], axis=1)
    return gelu(jnp.dot(stacked, weight, preferred_element_type=F32))


def ends_mixed(h, own, group_odd, one, two, middle, got_one, got_two, weight):
    channels = weight.shape[1]

    def block(upper):
        return weight[pl.ds(pl.multiple_of(jnp.where(upper, 2 * channels, 0), channels), channels), :]

    low, centre, high = block(group_odd), weight[channels : 2 * channels, :], block(jnp.logical_not(group_odd))
    three, single = own == 3, own == 1
    a, b, m, outer_a, outer_b = one[h], two[h], middle[h], got_one[h], got_two[h]
    inside_a = jnp.where(single, outer_b, jnp.where(three, m, b))
    inside_b = jnp.where(single, outer_a, jnp.where(three, m, a))
    value_a = mix(outer_a, a, inside_a, jnp.concatenate([high, centre, low], axis=0))
    value_b = mix(outer_b, b, inside_b, jnp.concatenate([low, centre, high], axis=0))
    return value_a, value_b


def mix_kernel(is_far, level_count, current, one, two, middle, got_one, got_two, weight, gain, middle_edge, new, edge):
    own, group_odd, lat_odd = here(level_count)
    first = far_row(lat_odd) if is_far else near_row(lat_odd)
    slots = plane_slots(own, group_odd)

    def each(h, carry):
        values = ends_mixed(h, own, group_odd, one, two, middle, got_one, got_two, weight)
        for plane, value in enumerate(values):
            x = (current[slots[plane], first + h].astype(F32) + value).astype(BF16)
            new[plane, h] = x
            edge[plane, h] = normed(x.astype(F32), gain[1:2, :])
        if not is_far:
            edge[2, h] = middle_edge[0, h]
        return carry

    lax.fori_loop(0, H, each, 0)


def last_kernel(level_count, current, one, two, middle, got_one, got_two, weight, out):
    own, group_odd, _ = here(level_count)

    def each(h, carry):
        for plane, value in enumerate(ends_mixed(h, own, group_odd, one, two, middle, got_one, got_two, weight)):
            out[plane, h] = (current[plane, h].astype(F32) + value).astype(BF16)
        return carry

    lax.fori_loop(0, H, each, 0)


def final_kernel(
    level_count, current, one, two, middle, got_one, got_two, weight, new_middle, near_ends, near_middle, out, rows, sems
):
    own, group_odd, lat_odd = here(level_count)
    slots = plane_slots(own, group_odd)
    zero = jnp.zeros(new_middle.shape[1:], BF16)

    def send(first, part):
        copies = [
            pltpu.make_async_copy(rows.at[slot, pl.ds(first, H)], out.at[slot, pl.ds(first, H)], sems.at[part, slot])
            for slot in range(out.shape[0])
        ]
        for copy in copies:
            copy.start()
        return copies

    near, far = near_row(lat_odd), far_row(lat_odd)
    for h in range(H):
        rows[1, near + h] = jnp.where(own == 3, near_middle[h], zero)
        rows[2, near + h] = zero
        rows[1, far + h] = jnp.where(own == 3, new_middle[h], zero)
        rows[2, far + h] = zero
        for plane in range(2):
            rows[slots[plane], near + h] = near_ends[plane, h]
    copies = send(near, 0)

    def each(h, carry):
        for plane, value in enumerate(ends_mixed(h, own, group_odd, one, two, middle, got_one, got_two, weight)):
            rows[slots[plane], far + h] = (current[plane, h].astype(F32) + value).astype(BF16)
        return carry

    lax.fori_loop(0, H, each, 0)
    for copy in copies + send(far, 1):
        copy.wait()


def pairs(count, first):
    found = [(i, i + 1) for i in range(first, count - 1, 2)]
    return found + [(j, i) for i, j in found]


def on_device(field, level_count, tap_rows, tap_lons, tap_values, norm_gain, disco_weight, vert_weight):
    slots, rows, lons, channels = field.shape
    lats, levs = lax.axis_size("lat"), lax.axis_size("lev")
    near_pairs, far_pairs = pairs(lats, 0), pairs(lats, 1)
    one_pairs, two_pairs = pairs(levs, 0), pairs(levs, 1)
    plane = jax.ShapeDtypeStruct((H, lons, channels), BF16)

    def edge(planes):
        return jax.ShapeDtypeStruct((planes, H, lons, channels), BF16)

    first_row = lax.axis_index("lat") * rows
    row_part = lax.dynamic_slice_in_dim(tap_rows, first_row, rows, 0)
    lon_part = lax.dynamic_slice_in_dim(tap_lons, first_row, rows, 0)
    value_part = lax.dynamic_slice_in_dim(tap_values, first_row, rows, 0).reshape(rows, TAPS * K)

    def maps_of(p, after=()):
        shape = jax.ShapeDtypeStruct((rows, TAPS * channels, channels), BF16)
        return call(tap_map_kernel, shape, [SMEM, VMEM], after=after, cost=10**10 if p == 0 else 1)(value_part, disco_weight[p])

    def padded(planes):
        return pltpu.VMEM((planes, rows + 2 * H, lons + 2 * PAD, channels), F32)

    hbm = pl.BlockSpec(memory_space=pltpu.HBM)
    scratch = [pltpu.VMEM((slots, H, lons, channels), BF16), pltpu.SemaphoreType.DMA((slots,))]

    def first_norm(is_far, after=()):
        kernel = functools.partial(norm_kernel, is_far)
        return call(kernel, edge(slots), [hbm, VMEM], scratch, after=after)(field, norm_gain)

    far = first_norm(True)
    near = first_norm(False, [far])
    near_got = lax.ppermute(near, "lat", near_pairs)
    far_got = lax.ppermute(far, "lat", far_pairs)
    maps = maps_of(0, [near])

    ends_edges = middle_edges = (far, near, far_got, near_got)
    middle_at = ((1, 1, 1), (1, 1, 1))
    ends_now, middle_now = (field, field), (field, field)
    for p in range(PASSES):
        last = p + 1 == PASSES
        done, after = [], []
        for is_far in (False, True):
            far, near, far_got, near_got = ends_edges
            one, two = call(
                functools.partial(ends_kernel, is_far, p == 0),
                [plane] * 2,
                [SMEM] * 3 + [VMEM] * 4,
                [padded(2)],
                after=after,
            )(level_count, row_part, lon_part, far, near, far_got if is_far else near_got, maps)
            got_one = lax.ppermute(one, "lev", one_pairs)
            got_two = lax.ppermute(two, "lev", two_pairs)
            far, near, far_got, near_got = middle_edges
            made = call(
                functools.partial(middle_kernel, is_far, middle_at[is_far]),
                [plane] * 2 + [edge(1)] * (not last),
                [SMEM] * 3 + [VMEM] * 9,
                [padded(1)],
            )(
                level_count, row_part, lon_part, far, near, far_got if is_far else near_got, maps,
                one, two, middle_now[is_far], vert_weight[p], norm_gain,
            )
            after = [made[0], one, two]
            done.append(((one, two, made[0], got_one, got_two, vert_weight[p]), made[1:]))
        (near_ends, near_made), (far_ends, far_made) = done
        if last:
            near_rows = call(last_kernel, edge(2), [SMEM] + [VMEM] * 7, after=after)(level_count, ends_now[0], *near_ends)
            return call(
                final_kernel,
                jax.ShapeDtypeStruct(field.shape, BF16),
                [SMEM] + [VMEM] * 10,
                [pltpu.VMEM(field.shape, BF16), pltpu.SemaphoreType.DMA((2, slots))],
                out_specs=hbm,
            )(level_count, ends_now[1], *far_ends, far_made[0], near_rows, near_made[0])
        middle_far = far_made[1]
        middle_far_got = lax.ppermute(middle_far, "lat", far_pairs)
        maps = maps_of(p + 1, after)
        new_near, near = call(functools.partial(mix_kernel, False), [edge(2), edge(3)], [SMEM] + [VMEM] * 9, after=[maps])(
            level_count, field, *near_ends, norm_gain, near_made[1]
        )
        near_got = lax.ppermute(near, "lat", near_pairs)
        new_far, far = call(functools.partial(mix_kernel, True), [edge(2), edge(2)], [SMEM] + [VMEM] * 9, after=[near], cost=10**10)(
            level_count, field, *far_ends, norm_gain, middle_far
        )
        far_got = lax.ppermute(far, "lat", far_pairs)
        ends_edges = (far, near, far_got, near_got)
        middle_edges = (middle_far, near, middle_far_got, near_got)
        middle_at = ((0, 2, 2), (0, 2, 0))
        ends_now, middle_now = (new_near, new_far), (near_made[0], far_made[0])


def solution(mesh):
    return jax.shard_map(
        on_device,
        mesh=mesh,
        in_specs=(P("lev", "lat", None, None), P(), P(), P(), P(), P(), P(), P()),
        out_specs=P("lev", "lat", None, None),
        check_vma=False,
    )
```

```python
import functools

import jax
import jax.numpy as jnp
from jax import lax
from jax.experimental import pallas as pl
from jax.experimental.pallas import tpu as pltpu
from jax.sharding import PartitionSpec as P

K = 4
TAPS = 8
H = 2
PASSES = 2
PAD = 8
EPSILON = 1e-06

BF16 = jnp.bfloat16
F32 = jnp.float32
VMEM = pl.BlockSpec(memory_space=pltpu.VMEM)
SMEM = pl.BlockSpec(memory_space=pltpu.SMEM)
LIMIT = 24 * 1024 * 1024


def call(kernel, out_shape, in_specs, scratch=(), after=(), cost=1, out_specs=None):
    many = isinstance(out_shape, (tuple, list))
    count, late = len(in_specs), len(after)

    def body(*refs):
        kernel(*refs[:count], *refs[count + late :])

    made = pl.pallas_call(
        body,
        out_shape=out_shape,
        in_specs=list(in_specs) + [pl.BlockSpec(memory_space=pl.ANY)] * late,
        out_specs=out_specs or ([VMEM] * len(out_shape) if many else VMEM),
        scratch_shapes=list(scratch),
        compiler_params=pltpu.CompilerParams(vmem_limit_bytes=LIMIT),
        cost_estimate=pl.CostEstimate(flops=cost, bytes_accessed=1, transcendentals=0),
    )
    return lambda *operands: made(*operands, *after)


def here():
    lat_odd = lax.axis_index("lat") % 2
    return (lax.axis_index("lev") + lat_odd) % 2 == 1, lat_odd


def own_levels(level_count):
    lanes = lax.broadcasted_iota(jnp.int32, level_count.shape, 1)
    return jnp.sum(jnp.where(lanes == lax.axis_index("lev"), level_count[...], 0), axis=1, keepdims=True)


def plane_slots(own, one_low):
    return jnp.where(one_low, 0, own - 1), jnp.where(one_low, own - 1, 0)


def choose(flag, yes, no):
    return jnp.where(jnp.broadcast_to(flag, yes.shape), yes, no)


def far_row(lat_odd):
    return H * lat_odd


def near_row(lat_odd):
    return H * (1 - lat_odd)


def normed(widened, gain):
    mean_square = jnp.mean(widened * widened, axis=-1, keepdims=True)
    return (widened * lax.rsqrt(mean_square + EPSILON) * gain).astype(BF16)


def norm_kernel(is_far, field, gain, out):
    _, lat_odd = here()
    first = far_row(lat_odd) if is_far else near_row(lat_odd)
    for slot in range(out.shape[0]):
        for h in range(H):
            out[slot, h] = normed(field[slot, first + h].astype(F32), gain[0:1, :])


def tap_map_kernel(values, weight, out):
    channels = weight.shape[-1]
    rows = values.shape[0]

    def one(index, carry):
        row = index // TAPS
        tap = index % TAPS
        total = None
        for k in range(K):
            part = values[row, tap * K + k] * weight[k * channels : (k + 1) * channels, :].astype(F32)
            total = part if total is None else total + part
        out[row, pl.ds(pl.multiple_of(tap * channels, channels), channels), :] = total.astype(BF16)
        return carry

    lax.fori_loop(0, rows * TAPS, one, 0)


def stage(scratch, place, refs, planes, firsts):
    for ref, plane, first in zip(refs, planes, firsts):
        lons = ref.shape[2]
        for h in range(H):
            value = ref[plane, h].astype(F32)
            scratch[place, first + h, pl.ds(PAD, lons), :] = value
            scratch[place, first + h, pl.ds(0, PAD), :] = value[lons - PAD :]
            scratch[place, first + h, pl.ds(PAD + lons, PAD), :] = value[:PAD]


def disco_rows(scratch, places, row, table, weights, lons):
    entries = table[pl.ds(row, 1), :]
    taps = [(row + entries[0, tap] + H, entries[0, TAPS + tap] + PAD) for tap in range(TAPS)]
    for place in places:
        parts = [scratch[place, source, pl.ds(start, lons), :].astype(BF16) for source, start in taps]
        total = jnp.dot(jnp.concatenate(parts, axis=1), weights[row], preferred_element_type=F32)
        yield total.astype(BF16)


def places_of(is_far):
    one_low, lat_odd = here()
    beyond = 3 * H * lat_odd if is_far else 3 * H * (1 - lat_odd)
    first = far_row(lat_odd) if is_far else near_row(lat_odd)
    return one_low, first, (H + far_row(lat_odd), H + near_row(lat_odd), beyond)


def ends_kernel(is_far, slotted, level_count, table, far, near, got, weights, one, two, scratch):
    one_low, first, at = places_of(is_far)
    for place in range(scratch.shape[0]):
        stage(scratch, place, (far, near, got), (place,) * 3, at)
    places = plane_slots(own_levels(level_count)[0, 0], one_low) if slotted else plane_slots(2, one_low)

    def each(h, carry):
        one[h], two[h] = disco_rows(scratch, places, first + h, table, weights, far.shape[2])
        return carry

    lax.fori_loop(0, H, each, 0, unroll=True)


def middle_kernel(is_far, planes, table, far, near, got, weights, one, two, current, mixing, gain, *rest):
    middle, new = rest[:2]
    scratch = rest[-1]
    one_low, first, at = places_of(is_far)
    stage(scratch, 0, (far, near, got), planes, at)

    def each(h, carry):
        (m,) = disco_rows(scratch, (0,), first + h, table, weights, far.shape[2])
        middle[h] = m
        below, above = jnp.where(one_low, one[h], two[h]), jnp.where(one_low, two[h], one[h])
        old = current[1, first + h] if len(current.shape) == 4 else current[h]
        x = (old.astype(F32) + mix(below, m, above, mixing[...])).astype(BF16)
        new[h] = x
        if len(rest) == 4:
            rest[2][0, h] = normed(x.astype(F32), gain[1:2, :])
        return carry

    lax.fori_loop(0, H, each, 0, unroll=True)


def gelu(v):
    return 0.5 * v * (1.0 + lax.erf(v * 0.7071067811865476))


def mix(below, disco, above, weight):
    stacked = jnp.concatenate([below, disco, above], axis=1)
    return gelu(jnp.dot(stacked, weight, preferred_element_type=F32))


def ends_mixed(h, own, one_low, one, two, middle, got_one, got_two, weight):
    channels = weight.shape[1]

    def block(upper):
        return weight[pl.ds(pl.multiple_of(jnp.where(upper, 2 * channels, 0), channels), channels), :]

    low, centre, high = block(one_low), weight[channels : 2 * channels, :], block(jnp.logical_not(one_low))
    a, b, m, outer_a, outer_b = one[h], two[h], middle[h], got_one[h], got_two[h]
    inside_a = choose(own == 1, outer_b, choose(own == 3, m, b))
    inside_b = choose(own == 1, outer_a, choose(own == 3, m, a))
    value_a = mix(outer_a, a, inside_a, jnp.concatenate([high, centre, low], axis=0))
    value_b = mix(outer_b, b, inside_b, jnp.concatenate([low, centre, high], axis=0))
    return value_a, value_b


def mix_kernel(is_far, level_count, current, one, two, middle, got_one, got_two, weight, gain, middle_edge, new, edge):
    own = own_levels(level_count)
    one_low, lat_odd = here()
    first = far_row(lat_odd) if is_far else near_row(lat_odd)

    def each(h, carry):
        low, centre, high = [current[slot, first + h] for slot in range(3)]
        top = choose(own == 3, high, choose(own == 2, centre, low))
        old = jnp.where(one_low, low, top), jnp.where(one_low, top, low)
        values = ends_mixed(h, own, one_low, one, two, middle, got_one, got_two, weight)
        for plane, value in enumerate(values):
            x = (old[plane].astype(F32) + value).astype(BF16)
            new[plane, h] = x
            edge[jnp.where(one_low, plane, 1 - plane), h] = normed(x.astype(F32), gain[1:2, :])
        if not is_far:
            edge[2, h] = middle_edge[0, h]
        return carry

    lax.fori_loop(0, H, each, 0, unroll=True)


def last_kernel(level_count, current, one, two, middle, got_one, got_two, weight, out):
    own = own_levels(level_count)
    one_low, _ = here()

    def each(h, carry):
        for plane, value in enumerate(ends_mixed(h, own, one_low, one, two, middle, got_one, got_two, weight)):
            out[plane, h] = (current[plane, h].astype(F32) + value).astype(BF16)
        return carry

    lax.fori_loop(0, H, each, 0, unroll=True)


def final_kernel(
    level_count, current, one, two, middle, got_one, got_two, weight, new_middle, near_ends, near_middle, out, rows, sems
):
    own = own_levels(level_count)
    one_low, lat_odd = here()
    near, far = near_row(lat_odd), far_row(lat_odd)

    copies = []

    def send(row, part):
        for slot in range(out.shape[0]):
            copies.append(pltpu.make_async_copy(rows.at[slot, row], out.at[slot, row], sems.at[part, slot]))
            copies[-1].start()

    def put(row, a, b, m):
        bottom, top = jnp.where(one_low, a, b), jnp.where(one_low, b, a)
        zero = jnp.zeros_like(m)
        rows[0, row] = bottom
        rows[1, row] = choose(own == 3, m, choose(own == 2, top, zero))
        rows[2, row] = choose(own == 3, top, zero)

    for h in range(H):
        put(near + h, near_ends[0, h], near_ends[1, h], near_middle[h])
        send(near + h, h)
    for h in range(H):
        values = ends_mixed(h, own, one_low, one, two, middle, got_one, got_two, weight)
        a, b = [(current[plane, h].astype(F32) + value).astype(BF16) for plane, value in enumerate(values)]
        put(far + h, a, b, new_middle[h])
        send(far + h, H + h)
    for copy in copies:
        copy.wait()


def pairs(count, first):
    found = [(i, i + 1) for i in range(first, count - 1, 2)]
    return found + [(j, i) for i, j in found]


def on_device(field, level_count, tap_rows, tap_lons, tap_values, norm_gain, disco_weight, vert_weight):
    slots, rows, lons, channels = field.shape
    lats, levs = lax.axis_size("lat"), lax.axis_size("lev")
    near_pairs, far_pairs = pairs(lats, 0), pairs(lats, 1)
    one_pairs, two_pairs = [
        [(a * lats + lat, b * lats + lat) for lat in range(lats) for a, b in pairs(levs, (lat + turn) % 2)] for turn in (0, 1)
    ]
    plane = jax.ShapeDtypeStruct((H, lons, channels), BF16)

    def edge(planes):
        return jax.ShapeDtypeStruct((planes, H, lons, channels), BF16)

    first_row = lax.axis_index("lat") * rows
    row_part = lax.dynamic_slice_in_dim(tap_rows, first_row, rows, 0)
    lon_part = lax.dynamic_slice_in_dim(tap_lons, first_row, rows, 0)
    table = jnp.concatenate([row_part, lon_part], axis=1)
    counts = level_count.reshape(1, -1)
    value_part = lax.dynamic_slice_in_dim(tap_values, first_row, rows, 0).reshape(rows, TAPS * K)

    def maps_of(p, after=()):
        shape = jax.ShapeDtypeStruct((rows, TAPS * channels, channels), BF16)
        return call(tap_map_kernel, shape, [SMEM, VMEM], after=after, cost=10**10 if p == 0 else 1)(value_part, disco_weight[p])

    def staged(planes):
        scratch = pltpu.VMEM((planes, rows + 2 * H, lons + 2 * PAD, channels), F32)
        return [scratch]

    hbm = pl.BlockSpec(memory_space=pltpu.HBM)

    def first_norm(is_far, after=()):
        kernel = functools.partial(norm_kernel, is_far)
        return call(kernel, edge(slots), [VMEM, VMEM], after=after)(field, norm_gain)

    far = first_norm(True)
    near = first_norm(False, [far])
    near_got = lax.ppermute(near, "lat", near_pairs)
    far_got = lax.ppermute(far, "lat", far_pairs)
    maps = maps_of(0, [near])

    ends_edges = middle_edges = (far, near, far_got, near_got)
    middle_at = ((1, 1, 1), (1, 1, 1))
    ends_now, middle_now = (field, field), (field, field)
    for p in range(PASSES):
        last = p + 1 == PASSES
        done, after = [], []
        for is_far in (False, True):
            far, near, far_got, near_got = ends_edges
            one, two = call(
                functools.partial(ends_kernel, is_far, p == 0),
                [plane] * 2,
                [VMEM] * 6,
                staged(slots if p == 0 else 2),
                after=after,
            )(counts, table, far, near, far_got if is_far else near_got, maps)
            got_one = lax.ppermute(one, ("lev", "lat"), one_pairs)
            got_two = lax.ppermute(two, ("lev", "lat"), two_pairs)
            far, near, far_got, near_got = middle_edges
            made = call(
                functools.partial(middle_kernel, is_far, middle_at[is_far]),
                [plane] * 2 + [edge(1)] * (not last),
                [VMEM] * 10,
                staged(1),
            )(
                table, far, near, far_got if is_far else near_got, maps,
                one, two, middle_now[is_far], vert_weight[p], norm_gain,
            )
            after = [made[0], one, two]
            done.append(((one, two, made[0], got_one, got_two, vert_weight[p]), made[1:]))
        (near_ends, near_made), (far_ends, far_made) = done
        if last:
            near_rows = call(last_kernel, edge(2), [VMEM] * 8, after=after)(counts, ends_now[0], *near_ends)
            return call(
                final_kernel,
                jax.ShapeDtypeStruct(field.shape, BF16),
                [VMEM] * 11,
                [pltpu.VMEM(field.shape, BF16), pltpu.SemaphoreType.DMA((2 * H, slots))],
                out_specs=hbm,
            )(counts, ends_now[1], *far_ends, far_made[0], near_rows, near_made[0])
        middle_far = far_made[1]
        middle_far_got = lax.ppermute(middle_far, "lat", far_pairs)
        maps = maps_of(p + 1, after)
        new_near, near = call(functools.partial(mix_kernel, False), [edge(2), edge(3)], [VMEM] * 10, after=[maps])(
            counts, field, *near_ends, norm_gain, near_made[1]
        )
        near_got = lax.ppermute(near, "lat", near_pairs)
        new_far, far = call(functools.partial(mix_kernel, True), [edge(2), edge(2)], [VMEM] * 10, after=[near], cost=10**10)(
            counts, field, *far_ends, norm_gain, middle_far
        )
        far_got = lax.ppermute(far, "lat", far_pairs)
        ends_edges = (far, near, far_got, near_got)
        middle_edges = (middle_far, near, middle_far_got, near_got)
        middle_at = ((0, 2, 2), (0, 2, 0))
        ends_now, middle_now = (new_near, new_far), (near_made[0], far_made[0])


def solution(mesh):
    return jax.shard_map(
        on_device,
        mesh=mesh,
        in_specs=(P("lev", "lat", None, None), P(), P(), P(), P(), P(), P(), P()),
        out_specs=P("lev", "lat", None, None),
        check_vma=False,
    )
```

```python
import functools

import jax
import jax.numpy as jnp
from jax import lax
from jax.experimental import pallas as pl
from jax.experimental.pallas import tpu as pltpu
from jax.sharding import PartitionSpec as P

K = 4
TAPS = 8
H = 2
PASSES = 2
PAD = 8
EPSILON = 1e-06

BF16 = jnp.bfloat16
F32 = jnp.float32
VMEM = pl.BlockSpec(memory_space=pltpu.VMEM)
SMEM = pl.BlockSpec(memory_space=pltpu.SMEM)
LIMIT = 24 * 1024 * 1024


def call(kernel, out_shape, in_specs, scratch=(), after=(), cost=1, out_specs=None):
    many = isinstance(out_shape, (tuple, list))
    count, late = len(in_specs), len(after)

    def body(*refs):
        kernel(*refs[:count], *refs[count + late :])

    made = pl.pallas_call(
        body,
        out_shape=out_shape,
        in_specs=list(in_specs) + [pl.BlockSpec(memory_space=pl.ANY)] * late,
        out_specs=out_specs or ([VMEM] * len(out_shape) if many else VMEM),
        scratch_shapes=list(scratch),
        compiler_params=pltpu.CompilerParams(vmem_limit_bytes=LIMIT),
        cost_estimate=pl.CostEstimate(flops=cost, bytes_accessed=1, transcendentals=0),
    )
    return lambda *operands: made(*operands, *after)


def here():
    lat_odd = lax.axis_index("lat") % 2
    return (lax.axis_index("lev") + lat_odd) % 2 == 1, lat_odd


def own_levels(level_count):
    lanes = lax.broadcasted_iota(jnp.int32, level_count.shape, 1)
    return jnp.sum(jnp.where(lanes == lax.axis_index("lev"), level_count[...], 0), axis=1, keepdims=True)


def plane_slots(own, one_low):
    return jnp.where(one_low, 0, own - 1), jnp.where(one_low, own - 1, 0)


def choose(flag, yes, no):
    return jnp.where(jnp.broadcast_to(flag, yes.shape), yes, no)


def far_row(lat_odd):
    return H * lat_odd


def near_row(lat_odd):
    return H * (1 - lat_odd)


def normed(widened, gain):
    mean_square = jnp.mean(widened * widened, axis=-1, keepdims=True)
    return (widened * lax.rsqrt(mean_square + EPSILON) * gain).astype(BF16)


def norm_kernel(is_far, field, gain, out):
    _, lat_odd = here()
    first = far_row(lat_odd) if is_far else near_row(lat_odd)
    for slot in range(out.shape[0]):
        for h in range(H):
            out[slot, h] = normed(field[slot, first + h].astype(F32), gain[0:1, :])


def tap_map_kernel(values, weight, out):
    channels = weight.shape[-1]
    rows = values.shape[0]

    def one(index, carry):
        row = index // TAPS
        tap = index % TAPS
        total = None
        for k in range(K):
            part = values[row, tap * K + k] * weight[k * channels : (k + 1) * channels, :].astype(F32)
            total = part if total is None else total + part
        out[row, pl.ds(pl.multiple_of(tap * channels, channels), channels), :] = total.astype(BF16)
        return carry

    lax.fori_loop(0, rows * TAPS, one, 0)


def stage(scratch, place, refs, planes, firsts):
    for ref, plane, first in zip(refs, planes, firsts):
        lons = ref.shape[2]
        for h in range(H):
            value = ref[plane, h].astype(F32)
            scratch[place, first + h, pl.ds(PAD, lons), :] = value
            scratch[place, first + h, pl.ds(0, PAD), :] = value[lons - PAD :]
            scratch[place, first + h, pl.ds(PAD + lons, PAD), :] = value[:PAD]


def disco_rows(scratch, places, row, table, weights, lons):
    entries = table[pl.ds(row, 1), :]
    taps = [(row + entries[0, tap] + H, entries[0, TAPS + tap] + PAD) for tap in range(TAPS)]
    for place in places:
        parts = [scratch[place, source, pl.ds(start, lons), :].astype(BF16) for source, start in taps]
        total = jnp.dot(jnp.concatenate(parts, axis=1), weights[row], preferred_element_type=F32)
        yield total.astype(BF16)


def places_of(is_far):
    one_low, lat_odd = here()
    beyond = 3 * H * lat_odd if is_far else 3 * H * (1 - lat_odd)
    first = far_row(lat_odd) if is_far else near_row(lat_odd)
    return one_low, first, (H + far_row(lat_odd), H + near_row(lat_odd), beyond)


def ends_kernel(is_far, slotted, level_count, table, far, near, got, weights, one, two, scratch):
    one_low, first, at = places_of(is_far)
    for place in range(scratch.shape[0]):
        stage(scratch, place, (far, near, got), (place,) * 3, at)
    places = plane_slots(own_levels(level_count)[0, 0], one_low) if slotted else plane_slots(2, one_low)

    def each(h, carry):
        one[h], two[h] = disco_rows(scratch, places, first + h, table, weights, far.shape[2])
        return carry

    lax.fori_loop(0, H, each, 0, unroll=True)


def middle_kernel(is_far, planes, table, far, near, got, weights, one, two, current, mixing, gain, *rest):
    middle, new = rest[:2]
    scratch = rest[-1]
    one_low, first, at = places_of(is_far)
    stage(scratch, 0, (far, near, got), planes, at)

    def each(h, carry):
        (m,) = disco_rows(scratch, (0,), first + h, table, weights, far.shape[2])
        middle[h] = m
        below, above = jnp.where(one_low, one[h], two[h]), jnp.where(one_low, two[h], one[h])
        old = current[1, first + h] if len(current.shape) == 4 else current[h]
        x = (old.astype(F32) + mix(below, m, above, mixing[...])).astype(BF16)
        new[h] = x
        if len(rest) == 4:
            rest[2][0, h] = normed(x.astype(F32), gain[1:2, :])
        return carry

    lax.fori_loop(0, H, each, 0, unroll=True)


def gelu(v):
    return 0.5 * v * (1.0 + lax.erf(v * 0.7071067811865476))


def mix(below, disco, above, weight):
    stacked = jnp.concatenate([below, disco, above], axis=1)
    return gelu(jnp.dot(stacked, weight, preferred_element_type=F32))


def ends_mixed(h, own, one_low, one, two, middle, got_one, got_two, weight):
    channels = weight.shape[1]

    def block(upper):
        return weight[pl.ds(pl.multiple_of(jnp.where(upper, 2 * channels, 0), channels), channels), :]

    low, centre, high = block(one_low), weight[channels : 2 * channels, :], block(jnp.logical_not(one_low))
    a, b, m, outer_a, outer_b = one[h], two[h], middle[h], got_one[h], got_two[h]
    inside_a = choose(own == 1, outer_b, choose(own == 3, m, b))
    inside_b = choose(own == 1, outer_a, choose(own == 3, m, a))
    value_a = mix(outer_a, a, inside_a, jnp.concatenate([high, centre, low], axis=0))
    value_b = mix(outer_b, b, inside_b, jnp.concatenate([low, centre, high], axis=0))
    return value_a, value_b


def mix_kernel(is_far, level_count, current, one, two, middle, got_one, got_two, weight, gain, middle_edge, new, edge):
    own = own_levels(level_count)
    one_low, lat_odd = here()
    first = far_row(lat_odd) if is_far else near_row(lat_odd)

    def each(h, carry):
        low, centre, high = [current[slot, first + h] for slot in range(3)]
        top = choose(own == 3, high, choose(own == 2, centre, low))
        old = jnp.where(one_low, low, top), jnp.where(one_low, top, low)
        values = ends_mixed(h, own, one_low, one, two, middle, got_one, got_two, weight)
        for plane, value in enumerate(values):
            x = (old[plane].astype(F32) + value).astype(BF16)
            new[plane, h] = x
            edge[jnp.where(one_low, plane, 1 - plane), h] = normed(x.astype(F32), gain[1:2, :])
        if not is_far:
            edge[2, h] = middle_edge[0, h]
        return carry

    lax.fori_loop(0, H, each, 0, unroll=True)


def last_kernel(level_count, current, one, two, middle, got_one, got_two, weight, out):
    own = own_levels(level_count)
    one_low, _ = here()

    def each(h, carry):
        for plane, value in enumerate(ends_mixed(h, own, one_low, one, two, middle, got_one, got_two, weight)):
            out[plane, h] = (current[plane, h].astype(F32) + value).astype(BF16)
        return carry

    lax.fori_loop(0, H, each, 0, unroll=True)


def final_kernel(
    level_count, current, one, two, middle, got_one, got_two, weight, new_middle, near_ends, near_middle, out, rows, sems
):
    own = own_levels(level_count)
    one_low, lat_odd = here()
    near, far = near_row(lat_odd), far_row(lat_odd)

    copies = []

    def send(row, part):
        for slot in range(out.shape[0]):
            copies.append(pltpu.make_async_copy(rows.at[slot, row], out.at[slot, row], sems.at[part, slot]))
            copies[-1].start()

    def put(row, a, b, m):
        bottom, top = jnp.where(one_low, a, b), jnp.where(one_low, b, a)
        zero = jnp.zeros_like(m)
        rows[0, row] = bottom
        rows[1, row] = choose(own == 3, m, choose(own == 2, top, zero))
        rows[2, row] = choose(own == 3, top, zero)

    for h in range(H):
        put(near + h, near_ends[0, h], near_ends[1, h], near_middle[h])
        send(near + h, h)
    for h in range(H):
        values = ends_mixed(h, own, one_low, one, two, middle, got_one, got_two, weight)
        a, b = [(current[plane, h].astype(F32) + value).astype(BF16) for plane, value in enumerate(values)]
        put(far + h, a, b, new_middle[h])
        send(far + h, H + h)
    for copy in copies:
        copy.wait()


def pairs(count, first):
    found = [(i, i + 1) for i in range(first, count - 1, 2)]
    return found + [(j, i) for i, j in found]


def on_device(field, level_count, tap_rows, tap_lons, tap_values, norm_gain, disco_weight, vert_weight):
    slots, rows, lons, channels = field.shape
    lats, levs = lax.axis_size("lat"), lax.axis_size("lev")
    near_pairs, far_pairs = pairs(lats, 0), pairs(lats, 1)
    one_pairs, two_pairs = [
        [(a * lats + lat, b * lats + lat) for lat in range(lats) for a, b in pairs(levs, (lat + turn) % 2)] for turn in (0, 1)
    ]
    plane = jax.ShapeDtypeStruct((H, lons, channels), BF16)

    def edge(planes):
        return jax.ShapeDtypeStruct((planes, H, lons, channels), BF16)

    first_row = lax.axis_index("lat") * rows
    row_part = lax.dynamic_slice_in_dim(tap_rows, first_row, rows, 0)
    lon_part = lax.dynamic_slice_in_dim(tap_lons, first_row, rows, 0)
    table = jnp.concatenate([row_part, lon_part], axis=1)
    counts = level_count.reshape(1, -1)
    value_part = lax.dynamic_slice_in_dim(tap_values, first_row, rows, 0).reshape(rows, TAPS * K)

    def maps_of(p, after=()):
        shape = jax.ShapeDtypeStruct((rows, TAPS * channels, channels), BF16)
        return call(tap_map_kernel, shape, [SMEM, VMEM], after=after, cost=10**10 if p == 0 else 1)(value_part, disco_weight[p])

    def staged(planes):
        scratch = pltpu.VMEM((planes, rows + 2 * H, lons + 2 * PAD, channels), F32)
        return [scratch]

    hbm = pl.BlockSpec(memory_space=pltpu.HBM)

    def first_norm(is_far, after=()):
        kernel = functools.partial(norm_kernel, is_far)
        return call(kernel, edge(slots), [VMEM, VMEM], after=after)(field, norm_gain)

    far = first_norm(True)
    near = first_norm(False, [far])
    near_got = lax.ppermute(near, "lat", near_pairs)
    far_got = lax.ppermute(far, "lat", far_pairs)
    maps = maps_of(0, [near])

    ends_edges = middle_edges = (far, near, far_got, near_got)
    middle_at = ((1, 1, 1), (1, 1, 1))
    ends_now, middle_now = (field, field), (field, field)
    for p in range(PASSES):
        last = p + 1 == PASSES
        def ends(is_far, after):
            far, near, far_got, near_got = ends_edges
            one, two = call(functools.partial(ends_kernel, is_far, p == 0), [plane] * 2, [VMEM] * 6, staged(slots if p == 0 else 2), after=after)(
                counts, table, far, near, far_got if is_far else near_got, maps
            )
            return one, two, lax.ppermute(one, ("lev", "lat"), one_pairs), lax.ppermute(two, ("lev", "lat"), two_pairs)

        def middles(is_far, one, two, after):
            far, near, far_got, near_got = middle_edges
            return call(
                functools.partial(middle_kernel, is_far, middle_at[is_far]),
                [plane] * 2 + [edge(1)] * (not last),
                [VMEM] * 10,
                staged(1),
                after=after,
            )(
                table, far, near, far_got if is_far else near_got, maps, one, two, middle_now[is_far], vert_weight[p], norm_gain
            )

        if last:
            near_one, near_two, *near_all_got = ends(False, [])
            far_one, far_two, *far_all_got = ends(True, [near_one, near_two])
            near_made = middles(False, near_one, near_two, [far_one, far_two])
            far_made = middles(True, far_one, far_two, [near_made[0], far_one, far_two])
        else:
            near_one, near_two, *near_all_got = ends(False, [])
            near_made = middles(False, near_one, near_two, [])
            far_one, far_two, *far_all_got = ends(True, [near_made[0], near_one, near_two])
            far_made = middles(True, far_one, far_two, [])
        after = [far_made[0], far_one, far_two]
        near_ends = (near_one, near_two, near_made[0], *near_all_got, vert_weight[p])
        far_ends = (far_one, far_two, far_made[0], *far_all_got, vert_weight[p])
        near_made, far_made = near_made[1:], far_made[1:]
        if last:
            near_rows = call(last_kernel, edge(2), [VMEM] * 8, after=after)(counts, ends_now[0], *near_ends)
            return call(
                final_kernel,
                jax.ShapeDtypeStruct(field.shape, BF16),
                [VMEM] * 11,
                [pltpu.VMEM(field.shape, BF16), pltpu.SemaphoreType.DMA((2 * H, slots))],
                out_specs=hbm,
            )(counts, ends_now[1], *far_ends, far_made[0], near_rows, near_made[0])
        middle_far = far_made[1]
        middle_far_got = lax.ppermute(middle_far, "lat", far_pairs)
        maps = maps_of(p + 1, after)
        new_near, near = call(functools.partial(mix_kernel, False), [edge(2), edge(3)], [VMEM] * 10, after=[maps])(
            counts, field, *near_ends, norm_gain, near_made[1]
        )
        near_got = lax.ppermute(near, "lat", near_pairs)
        new_far, far = call(functools.partial(mix_kernel, True), [edge(2), edge(2)], [VMEM] * 10, after=[near], cost=10**10)(
            counts, field, *far_ends, norm_gain, middle_far
        )
        far_got = lax.ppermute(far, "lat", far_pairs)
        ends_edges = (far, near, far_got, near_got)
        middle_edges = (middle_far, near, middle_far_got, near_got)
        middle_at = ((0, 2, 2), (0, 2, 0))
        ends_now, middle_now = (new_near, new_far), (near_made[0], far_made[0])


def solution(mesh):
    return jax.shard_map(
        on_device,
        mesh=mesh,
        in_specs=(P("lev", "lat", None, None), P(), P(), P(), P(), P(), P(), P()),
        out_specs=P("lev", "lat", None, None),
        check_vma=False,
    )
```

```python
import functools

import jax
import jax.numpy as jnp
from jax import lax
from jax.experimental import pallas as pl
from jax.experimental.pallas import tpu as pltpu
from jax.sharding import PartitionSpec as P

K = 4
TAPS = 8
H = 2
PASSES = 2
PAD = 8
EPSILON = 1e-06

BF16 = jnp.bfloat16
F32 = jnp.float32
VMEM = pl.BlockSpec(memory_space=pltpu.VMEM)
SMEM = pl.BlockSpec(memory_space=pltpu.SMEM)
LIMIT = 24 * 1024 * 1024


def call(kernel, out_shape, in_specs, scratch=(), after=(), cost=1, out_specs=None):
    many = isinstance(out_shape, (tuple, list))
    count, late = len(in_specs), len(after)

    def body(*refs):
        kernel(*refs[:count], *refs[count + late :])

    made = pl.pallas_call(
        body,
        out_shape=out_shape,
        in_specs=list(in_specs) + [pl.BlockSpec(memory_space=pl.ANY)] * late,
        out_specs=out_specs or ([VMEM] * len(out_shape) if many else VMEM),
        scratch_shapes=list(scratch),
        compiler_params=pltpu.CompilerParams(vmem_limit_bytes=LIMIT),
        cost_estimate=pl.CostEstimate(flops=cost, bytes_accessed=1, transcendentals=0),
    )
    return lambda *operands: made(*operands, *after)


def here():
    lat_odd = lax.axis_index("lat") % 2
    lat = lax.axis_index("lat")
    return (lax.axis_index("lev") + lat + lat // 2) % 2 == 1, lat_odd


def own_levels(level_count):
    lanes = lax.broadcasted_iota(jnp.int32, level_count.shape, 1)
    return jnp.sum(jnp.where(lanes == lax.axis_index("lev"), level_count[...], 0), axis=1, keepdims=True)


def plane_slots(own, one_low):
    return jnp.where(one_low, 0, own - 1), jnp.where(one_low, own - 1, 0)


def choose(flag, yes, no):
    return jnp.where(jnp.broadcast_to(flag, yes.shape), yes, no)


def far_row(lat_odd):
    return H * lat_odd


def near_row(lat_odd):
    return H * (1 - lat_odd)


def normed(widened, gain):
    mean_square = jnp.mean(widened * widened, axis=-1, keepdims=True)
    return (widened * lax.rsqrt(mean_square + EPSILON) * gain).astype(BF16)


def norm_kernel(is_far, field, gain, out):
    _, lat_odd = here()
    first = far_row(lat_odd) if is_far else near_row(lat_odd)
    for slot in range(out.shape[0]):
        for h in range(H):
            out[slot, h] = normed(field[slot, first + h].astype(F32), gain[0:1, :])


def tap_map_kernel(values, weight, out):
    channels = weight.shape[-1]
    rows = values.shape[0]

    def one(index, carry):
        row = index // TAPS
        tap = index % TAPS
        total = None
        for k in range(K):
            part = values[row, tap * K + k] * weight[k * channels : (k + 1) * channels, :].astype(F32)
            total = part if total is None else total + part
        out[row, pl.ds(pl.multiple_of(tap * channels, channels), channels), :] = total.astype(BF16)
        return carry

    lax.fori_loop(0, rows * TAPS, one, 0)


def stage(scratch, place, refs, planes, firsts):
    for ref, plane, first in zip(refs, planes, firsts):
        lons = ref.shape[2]
        for h in range(H):
            value = ref[plane, h].astype(F32)
            scratch[place, first + h, pl.ds(PAD, lons), :] = value
            scratch[place, first + h, pl.ds(0, PAD), :] = value[lons - PAD :]
            scratch[place, first + h, pl.ds(PAD + lons, PAD), :] = value[:PAD]


def disco_rows(scratch, places, row, table, weights, lons):
    entries = table[pl.ds(row, 1), :]
    taps = [(row + entries[0, tap] + H, entries[0, TAPS + tap] + PAD) for tap in range(TAPS)]
    for place in places:
        parts = [scratch[place, source, pl.ds(start, lons), :].astype(BF16) for source, start in taps]
        total = jnp.dot(jnp.concatenate(parts, axis=1), weights[row], preferred_element_type=F32)
        yield total.astype(BF16)


def places_of(is_far):
    one_low, lat_odd = here()
    beyond = 3 * H * lat_odd if is_far else 3 * H * (1 - lat_odd)
    first = far_row(lat_odd) if is_far else near_row(lat_odd)
    return one_low, first, (H + far_row(lat_odd), H + near_row(lat_odd), beyond)


def ends_kernel(is_far, slotted, level_count, table, far, near, got, weights, one, two, scratch):
    one_low, first, at = places_of(is_far)
    for place in range(scratch.shape[0]):
        stage(scratch, place, (far, near, got), (place,) * 3, at)
    places = plane_slots(own_levels(level_count)[0, 0], one_low) if slotted else plane_slots(2, one_low)

    def each(h, carry):
        one[h], two[h] = disco_rows(scratch, places, first + h, table, weights, far.shape[2])
        return carry

    lax.fori_loop(0, H, each, 0, unroll=True)


def middle_kernel(is_far, planes, table, far, near, got, weights, one, two, current, mixing, gain, *rest):
    middle, new = rest[:2]
    scratch = rest[-1]
    one_low, first, at = places_of(is_far)
    stage(scratch, 0, (far, near, got), planes, at)

    def each(h, carry):
        (m,) = disco_rows(scratch, (0,), first + h, table, weights, far.shape[2])
        middle[h] = m
        below, above = jnp.where(one_low, one[h], two[h]), jnp.where(one_low, two[h], one[h])
        old = current[1, first + h] if len(current.shape) == 4 else current[h]
        x = (old.astype(F32) + mix(below, m, above, mixing[...])).astype(BF16)
        new[h] = x
        if len(rest) == 4:
            rest[2][0, h] = normed(x.astype(F32), gain[1:2, :])
        return carry

    lax.fori_loop(0, H, each, 0, unroll=True)


def gelu(v):
    return 0.5 * v * (1.0 + lax.erf(v * 0.7071067811865476))


def mix(below, disco, above, weight):
    stacked = jnp.concatenate([below, disco, above], axis=1)
    return gelu(jnp.dot(stacked, weight, preferred_element_type=F32))


def ends_mixed(h, own, one_low, one, two, middle, got_one, got_two, weight):
    channels = weight.shape[1]

    def block(upper):
        return weight[pl.ds(pl.multiple_of(jnp.where(upper, 2 * channels, 0), channels), channels), :]

    low, centre, high = block(one_low), weight[channels : 2 * channels, :], block(jnp.logical_not(one_low))
    a, b, m, outer_a, outer_b = one[h], two[h], middle[h], got_one[h], got_two[h]
    inside_a = choose(own == 1, outer_b, choose(own == 3, m, b))
    inside_b = choose(own == 1, outer_a, choose(own == 3, m, a))
    value_a = mix(outer_a, a, inside_a, jnp.concatenate([high, centre, low], axis=0))
    value_b = mix(outer_b, b, inside_b, jnp.concatenate([low, centre, high], axis=0))
    return value_a, value_b


def mix_kernel(is_far, level_count, current, one, two, middle, got_one, got_two, weight, gain, middle_edge, new, edge):
    own = own_levels(level_count)
    one_low, lat_odd = here()
    first = far_row(lat_odd) if is_far else near_row(lat_odd)

    def each(h, carry):
        low, centre, high = [current[slot, first + h] for slot in range(3)]
        top = choose(own == 3, high, choose(own == 2, centre, low))
        old = jnp.where(one_low, low, top), jnp.where(one_low, top, low)
        values = ends_mixed(h, own, one_low, one, two, middle, got_one, got_two, weight)
        for plane, value in enumerate(values):
            x = (old[plane].astype(F32) + value).astype(BF16)
            new[plane, h] = x
            edge[jnp.where(one_low, plane, 1 - plane), h] = normed(x.astype(F32), gain[1:2, :])
        if not is_far:
            edge[2, h] = middle_edge[0, h]
        return carry

    lax.fori_loop(0, H, each, 0, unroll=True)


def last_kernel(level_count, current, one, two, middle, got_one, got_two, weight, out):
    own = own_levels(level_count)
    one_low, _ = here()

    def each(h, carry):
        for plane, value in enumerate(ends_mixed(h, own, one_low, one, two, middle, got_one, got_two, weight)):
            out[plane, h] = (current[plane, h].astype(F32) + value).astype(BF16)
        return carry

    lax.fori_loop(0, H, each, 0, unroll=True)


def final_kernel(
    level_count, current, one, two, middle, got_one, got_two, weight, new_middle, near_ends, near_middle, out, rows, sems
):
    own = own_levels(level_count)
    one_low, lat_odd = here()
    near, far = near_row(lat_odd), far_row(lat_odd)

    copies = []

    def send(row, part):
        for slot in range(out.shape[0]):
            copies.append(pltpu.make_async_copy(rows.at[slot, row], out.at[slot, row], sems.at[part, slot]))
            copies[-1].start()

    def put(row, a, b, m):
        bottom, top = jnp.where(one_low, a, b), jnp.where(one_low, b, a)
        zero = jnp.zeros_like(m)
        rows[0, row] = bottom
        rows[1, row] = choose(own == 3, m, choose(own == 2, top, zero))
        rows[2, row] = choose(own == 3, top, zero)

    for h in range(H):
        put(near + h, near_ends[0, h], near_ends[1, h], near_middle[h])
        send(near + h, h)
    for h in range(H):
        values = ends_mixed(h, own, one_low, one, two, middle, got_one, got_two, weight)
        a, b = [(current[plane, h].astype(F32) + value).astype(BF16) for plane, value in enumerate(values)]
        put(far + h, a, b, new_middle[h])
        send(far + h, H + h)
    for copy in copies:
        copy.wait()


def pairs(count, first):
    found = [(i, i + 1) for i in range(first, count - 1, 2)]
    return found + [(j, i) for i, j in found]


def on_device(field, level_count, tap_rows, tap_lons, tap_values, norm_gain, disco_weight, vert_weight):
    slots, rows, lons, channels = field.shape
    lats, levs = lax.axis_size("lat"), lax.axis_size("lev")
    near_pairs, far_pairs = pairs(lats, 0), pairs(lats, 1)
    one_pairs, two_pairs = [
        [(a * lats + lat, b * lats + lat) for lat in range(lats) for a, b in pairs(levs, (lat + lat // 2 + turn) % 2)] for turn in (0, 1)
    ]
    plane = jax.ShapeDtypeStruct((H, lons, channels), BF16)

    def edge(planes):
        return jax.ShapeDtypeStruct((planes, H, lons, channels), BF16)

    first_row = lax.axis_index("lat") * rows
    row_part = lax.dynamic_slice_in_dim(tap_rows, first_row, rows, 0)
    lon_part = lax.dynamic_slice_in_dim(tap_lons, first_row, rows, 0)
    table = jnp.concatenate([row_part, lon_part], axis=1)
    counts = level_count.reshape(1, -1)
    value_part = lax.dynamic_slice_in_dim(tap_values, first_row, rows, 0).reshape(rows, TAPS * K)

    def maps_of(p, after=()):
        shape = jax.ShapeDtypeStruct((rows, TAPS * channels, channels), BF16)
        return call(tap_map_kernel, shape, [SMEM, VMEM], after=after, cost=10**10 if p == 0 else 1)(value_part, disco_weight[p])

    def staged(planes):
        scratch = pltpu.VMEM((planes, rows + 2 * H, lons + 2 * PAD, channels), F32)
        return [scratch]

    hbm = pl.BlockSpec(memory_space=pltpu.HBM)

    def first_norm(is_far, after=()):
        kernel = functools.partial(norm_kernel, is_far)
        return call(kernel, edge(slots), [VMEM, VMEM], after=after)(field, norm_gain)

    far = first_norm(True)
    near = first_norm(False, [far])
    near_got = lax.ppermute(near, "lat", near_pairs)
    far_got = lax.ppermute(far, "lat", far_pairs)
    maps = maps_of(0, [near])

    ends_edges = middle_edges = (far, near, far_got, near_got)
    middle_at = ((1, 1, 1), (1, 1, 1))
    ends_now, middle_now = (field, field), (field, field)
    for p in range(PASSES):
        last = p + 1 == PASSES
        def ends(is_far, after):
            far, near, far_got, near_got = ends_edges
            one, two = call(functools.partial(ends_kernel, is_far, p == 0), [plane] * 2, [VMEM] * 6, staged(slots if p == 0 else 2), after=after)(
                counts, table, far, near, far_got if is_far else near_got, maps
            )
            return one, two, lax.ppermute(one, ("lev", "lat"), one_pairs), lax.ppermute(two, ("lev", "lat"), two_pairs)

        def middles(is_far, one, two, after):
            far, near, far_got, near_got = middle_edges
            return call(
                functools.partial(middle_kernel, is_far, middle_at[is_far]),
                [plane] * 2 + [edge(1)] * (not last),
                [VMEM] * 10,
                staged(1),
                after=after,
            )(
                table, far, near, far_got if is_far else near_got, maps, one, two, middle_now[is_far], vert_weight[p], norm_gain
            )

        if last:
            near_one, near_two, *near_all_got = ends(False, [])
            far_one, far_two, *far_all_got = ends(True, [near_one, near_two])
            near_made = middles(False, near_one, near_two, [far_one, far_two])
            far_made = middles(True, far_one, far_two, [near_made[0], far_one, far_two])
        else:
            near_one, near_two, *near_all_got = ends(False, [])
            near_made = middles(False, near_one, near_two, [])
            far_one, far_two, *far_all_got = ends(True, [near_made[0], near_one, near_two])
            far_made = middles(True, far_one, far_two, [])
        after = [far_made[0], far_one, far_two]
        near_ends = (near_one, near_two, near_made[0], *near_all_got, vert_weight[p])
        far_ends = (far_one, far_two, far_made[0], *far_all_got, vert_weight[p])
        near_made, far_made = near_made[1:], far_made[1:]
        if last:
            near_rows = call(last_kernel, edge(2), [VMEM] * 8, after=after)(counts, ends_now[0], *near_ends)
            return call(
                final_kernel,
                jax.ShapeDtypeStruct(field.shape, BF16),
                [VMEM] * 11,
                [pltpu.VMEM(field.shape, BF16), pltpu.SemaphoreType.DMA((2 * H, slots))],
                out_specs=hbm,
            )(counts, ends_now[1], *far_ends, far_made[0], near_rows, near_made[0])
        middle_far = far_made[1]
        middle_far_got = lax.ppermute(middle_far, "lat", far_pairs)
        maps = maps_of(p + 1, after)
        new_near, near = call(functools.partial(mix_kernel, False), [edge(2), edge(3)], [VMEM] * 10, after=[maps])(
            counts, field, *near_ends, norm_gain, near_made[1]
        )
        near_got = lax.ppermute(near, "lat", near_pairs)
        new_far, far = call(functools.partial(mix_kernel, True), [edge(2), edge(2)], [VMEM] * 10, after=[near], cost=10**10)(
            counts, field, *far_ends, norm_gain, middle_far
        )
        far_got = lax.ppermute(far, "lat", far_pairs)
        ends_edges = (far, near, far_got, near_got)
        middle_edges = (middle_far, near, middle_far_got, near_got)
        middle_at = ((0, 2, 2), (0, 2, 0))
        ends_now, middle_now = (new_near, new_far), (near_made[0], far_made[0])


def solution(mesh):
    return jax.shard_map(
        on_device,
        mesh=mesh,
        in_specs=(P("lev", "lat", None, None), P(), P(), P(), P(), P(), P(), P()),
        out_specs=P("lev", "lat", None, None),
        check_vma=False,
    )
```

```python
import functools

import jax
import jax.numpy as jnp
from jax import lax
from jax.experimental import pallas as pl
from jax.experimental.pallas import tpu as pltpu
from jax.sharding import PartitionSpec as P

K = 4
TAPS = 8
H = 2
PASSES = 2
PAD = 8
EPSILON = 1e-06

BF16 = jnp.bfloat16
F32 = jnp.float32
VMEM = pl.BlockSpec(memory_space=pltpu.VMEM)
SMEM = pl.BlockSpec(memory_space=pltpu.SMEM)
LIMIT = 24 * 1024 * 1024


def call(kernel, out_shape, in_specs, scratch=(), after=(), cost=1, out_specs=None):
    many = isinstance(out_shape, (tuple, list))
    count, late = len(in_specs), len(after)

    def body(*refs):
        kernel(*refs[:count], *refs[count + late :])

    made = pl.pallas_call(
        body,
        out_shape=out_shape,
        in_specs=list(in_specs) + [pl.BlockSpec(memory_space=pl.ANY)] * late,
        out_specs=out_specs or ([VMEM] * len(out_shape) if many else VMEM),
        scratch_shapes=list(scratch),
        compiler_params=pltpu.CompilerParams(vmem_limit_bytes=LIMIT),
        cost_estimate=pl.CostEstimate(flops=cost, bytes_accessed=1, transcendentals=0),
    )
    return lambda *operands: made(*operands, *after)


def here():
    lat_odd = lax.axis_index("lat") % 2
    lat = lax.axis_index("lat")
    return (lax.axis_index("lev") + lat + lat // 2) % 2 == 1, lat_odd


def own_levels(level_count):
    lanes = lax.broadcasted_iota(jnp.int32, level_count.shape, 1)
    return jnp.sum(jnp.where(lanes == lax.axis_index("lev"), level_count[...], 0), axis=1, keepdims=True)


def plane_slots(own, one_low):
    return jnp.where(one_low, 0, own - 1), jnp.where(one_low, own - 1, 0)


def choose(flag, yes, no):
    return jnp.where(jnp.broadcast_to(flag, yes.shape), yes, no)


def far_row(lat_odd):
    return H * lat_odd


def near_row(lat_odd):
    return H * (1 - lat_odd)


def normed(widened, gain):
    mean_square = jnp.mean(widened * widened, axis=-1, keepdims=True)
    return (widened * lax.rsqrt(mean_square + EPSILON) * gain).astype(BF16)


def norm_kernel(is_far, field, gain, out):
    _, lat_odd = here()
    first = far_row(lat_odd) if is_far else near_row(lat_odd)
    for slot in range(out.shape[0]):
        for h in range(H):
            out[slot, h] = normed(field[slot, first + h].astype(F32), gain[0:1, :])


def tap_map_kernel(values, weight, out):
    channels = weight.shape[-1]
    rows = values.shape[0]

    def one(index, carry):
        row = index // TAPS
        tap = index % TAPS
        total = None
        for k in range(K):
            part = values[row, tap * K + k] * weight[k * channels : (k + 1) * channels, :].astype(F32)
            total = part if total is None else total + part
        out[row, pl.ds(pl.multiple_of(tap * channels, channels), channels), :] = total.astype(BF16)
        return carry

    lax.fori_loop(0, rows * TAPS, one, 0)


def stage(scratch, place, refs, planes, firsts):
    for ref, plane, first in zip(refs, planes, firsts):
        lons = ref.shape[2]
        for h in range(H):
            value = ref[plane, h].astype(F32)
            scratch[place, first + h, pl.ds(PAD, lons), :] = value
            scratch[place, first + h, pl.ds(0, PAD), :] = value[lons - PAD :]
            scratch[place, first + h, pl.ds(PAD + lons, PAD), :] = value[:PAD]


def disco_rows(scratch, places, row, table, weights, lons):
    entries = table[pl.ds(row, 1), :]
    taps = [(row + entries[0, tap] + H, entries[0, TAPS + tap] + PAD) for tap in range(TAPS)]
    for place in places:
        parts = [scratch[place, source, pl.ds(start, lons), :].astype(BF16) for source, start in taps]
        total = jnp.dot(jnp.concatenate(parts, axis=1), weights[row], preferred_element_type=F32)
        yield total.astype(BF16)


def places_of(is_far):
    one_low, lat_odd = here()
    beyond = 3 * H * lat_odd if is_far else 3 * H * (1 - lat_odd)
    first = far_row(lat_odd) if is_far else near_row(lat_odd)
    return one_low, first, (H + far_row(lat_odd), H + near_row(lat_odd), beyond)


def ends_kernel(is_far, slotted, level_count, table, far, near, got, weights, one, two, scratch):
    one_low, first, at = places_of(is_far)
    for place in range(scratch.shape[0]):
        stage(scratch, place, (far, near, got), (place,) * 3, at)
    places = plane_slots(own_levels(level_count)[0, 0], one_low) if slotted else plane_slots(2, one_low)

    def each(h, carry):
        one[h], two[h] = disco_rows(scratch, places, first + h, table, weights, far.shape[2])
        return carry

    lax.fori_loop(0, H, each, 0, unroll=True)


def middle_kernel(is_far, planes, table, far, near, got, weights, one, two, current, mixing, gain, *rest):
    middle, new = rest[:2]
    scratch = rest[-1]
    one_low, first, at = places_of(is_far)
    stage(scratch, 0, (far, near, got), planes, at)

    def each(h, carry):
        (m,) = disco_rows(scratch, (0,), first + h, table, weights, far.shape[2])
        middle[h] = m
        below, above = jnp.where(one_low, one[h], two[h]), jnp.where(one_low, two[h], one[h])
        old = current[1, first + h] if len(current.shape) == 4 else current[h]
        x = (old.astype(F32) + mix(below, m, above, mixing[...])).astype(BF16)
        new[h] = x
        if len(rest) == 4:
            rest[2][0, h] = normed(x.astype(F32), gain[1:2, :])
        return carry

    lax.fori_loop(0, H, each, 0, unroll=True)


def gelu(v):
    return 0.5 * v * (1.0 + lax.erf(v * 0.7071067811865476))


def mix(below, disco, above, weight):
    stacked = jnp.concatenate([below, disco, above], axis=1)
    return gelu(jnp.dot(stacked, weight, preferred_element_type=F32))


def ends_mixed(h, own, one_low, one, two, middle, got_one, got_two, weight):
    channels = weight.shape[1]

    def block(upper):
        return weight[pl.ds(pl.multiple_of(jnp.where(upper, 2 * channels, 0), channels), channels), :]

    low, centre, high = block(one_low), weight[channels : 2 * channels, :], block(jnp.logical_not(one_low))
    a, b, m, outer_a, outer_b = one[h], two[h], middle[h], got_one[h], got_two[h]
    inside_a = choose(own == 1, outer_b, choose(own == 3, m, b))
    inside_b = choose(own == 1, outer_a, choose(own == 3, m, a))
    value_a = mix(outer_a, a, inside_a, jnp.concatenate([high, centre, low], axis=0))
    value_b = mix(outer_b, b, inside_b, jnp.concatenate([low, centre, high], axis=0))
    return value_a, value_b


def mix_kernel(is_far, level_count, current, one, two, middle, got_one, got_two, weight, gain, middle_edge, new, edge):
    own = own_levels(level_count)
    one_low, lat_odd = here()
    first = far_row(lat_odd) if is_far else near_row(lat_odd)

    def each(h, carry):
        low, centre, high = [current[slot, first + h] for slot in range(3)]
        top = choose(own == 3, high, choose(own == 2, centre, low))
        old = jnp.where(one_low, low, top), jnp.where(one_low, top, low)
        values = ends_mixed(h, own, one_low, one, two, middle, got_one, got_two, weight)
        for plane, value in enumerate(values):
            x = (old[plane].astype(F32) + value).astype(BF16)
            new[plane, h] = x
            edge[jnp.where(one_low, plane, 1 - plane), h] = normed(x.astype(F32), gain[1:2, :])
        if not is_far:
            edge[2, h] = middle_edge[0, h]
        return carry

    lax.fori_loop(0, H, each, 0, unroll=True)


def put(rows, row, own, one_low, a, b, m):
    bottom, top = jnp.where(one_low, a, b), jnp.where(one_low, b, a)
    zero = jnp.zeros_like(m)
    rows[0, row] = bottom
    rows[1, row] = choose(own == 3, m, choose(own == 2, top, zero))
    rows[2, row] = choose(own == 3, top, zero)


def last_kernel(level_count, current, one, two, middle, got_one, got_two, weight, new_middle, out):
    own = own_levels(level_count)
    one_low, _ = here()
    for h in range(H):
        values = ends_mixed(h, own, one_low, one, two, middle, got_one, got_two, weight)
        a, b = [(current[plane, h].astype(F32) + value).astype(BF16) for plane, value in enumerate(values)]
        put(out, h, own, one_low, a, b, new_middle[h])


def final_kernel(
    level_count, current, one, two, middle, got_one, got_two, weight, new_middle, near_rows, out, rows, sems
):
    own = own_levels(level_count)
    one_low, lat_odd = here()
    near, far = near_row(lat_odd), far_row(lat_odd)

    copies = []

    def send(source, row, part):
        for slot in range(out.shape[0]):
            copies.append(pltpu.make_async_copy(source.at[slot], out.at[slot, row], sems.at[part, slot]))
            copies[-1].start()

    for h in range(H):
        send(near_rows.at[:, h], near + h, h)
    for h in range(H):
        values = ends_mixed(h, own, one_low, one, two, middle, got_one, got_two, weight)
        a, b = [(current[plane, h].astype(F32) + value).astype(BF16) for plane, value in enumerate(values)]
        put(rows, h, own, one_low, a, b, new_middle[h])
        send(rows.at[:, h], far + h, H + h)
    for copy in copies:
        copy.wait()


def pairs(count, first):
    found = [(i, i + 1) for i in range(first, count - 1, 2)]
    return found + [(j, i) for i, j in found]


def on_device(field, level_count, tap_rows, tap_lons, tap_values, norm_gain, disco_weight, vert_weight):
    slots, rows, lons, channels = field.shape
    lats, levs = lax.axis_size("lat"), lax.axis_size("lev")
    near_pairs, far_pairs = pairs(lats, 0), pairs(lats, 1)
    one_pairs, two_pairs = [
        [(a * lats + lat, b * lats + lat) for lat in range(lats) for a, b in pairs(levs, (lat + lat // 2 + turn) % 2)] for turn in (0, 1)
    ]
    plane = jax.ShapeDtypeStruct((H, lons, channels), BF16)

    def edge(planes):
        return jax.ShapeDtypeStruct((planes, H, lons, channels), BF16)

    first_row = lax.axis_index("lat") * rows
    row_part = lax.dynamic_slice_in_dim(tap_rows, first_row, rows, 0)
    lon_part = lax.dynamic_slice_in_dim(tap_lons, first_row, rows, 0)
    table = jnp.concatenate([row_part, lon_part], axis=1)
    counts = level_count.reshape(1, -1)
    value_part = lax.dynamic_slice_in_dim(tap_values, first_row, rows, 0).reshape(rows, TAPS * K)

    def maps_of(p, after=()):
        shape = jax.ShapeDtypeStruct((rows, TAPS * channels, channels), BF16)
        return call(tap_map_kernel, shape, [SMEM, VMEM], after=after, cost=10**10 if p == 0 else 1)(value_part, disco_weight[p])

    def staged(planes):
        scratch = pltpu.VMEM((planes, rows + 2 * H, lons + 2 * PAD, channels), F32)
        return [scratch]

    hbm = pl.BlockSpec(memory_space=pltpu.HBM)

    def first_norm(is_far, after=()):
        kernel = functools.partial(norm_kernel, is_far)
        return call(kernel, edge(slots), [VMEM, VMEM], after=after)(field, norm_gain)

    far = first_norm(True)
    near = first_norm(False, [far])
    near_got = lax.ppermute(near, "lat", near_pairs)
    far_got = lax.ppermute(far, "lat", far_pairs)
    maps = maps_of(0, [near])

    ends_edges = middle_edges = (far, near, far_got, near_got)
    middle_at = ((1, 1, 1), (1, 1, 1))
    ends_now, middle_now = (field, field), (field, field)
    for p in range(PASSES):
        last = p + 1 == PASSES
        def ends(is_far, after):
            far, near, far_got, near_got = ends_edges
            one, two = call(functools.partial(ends_kernel, is_far, p == 0), [plane] * 2, [VMEM] * 6, staged(slots if p == 0 else 2), after=after)(
                counts, table, far, near, far_got if is_far else near_got, maps
            )
            return one, two, lax.ppermute(one, ("lev", "lat"), one_pairs), lax.ppermute(two, ("lev", "lat"), two_pairs)

        def middles(is_far, one, two, after):
            far, near, far_got, near_got = middle_edges
            return call(
                functools.partial(middle_kernel, is_far, middle_at[is_far]),
                [plane] * 2 + [edge(1)] * (not last),
                [VMEM] * 10,
                staged(1),
                after=after,
            )(
                table, far, near, far_got if is_far else near_got, maps, one, two, middle_now[is_far], vert_weight[p], norm_gain
            )

        if last:
            near_one, near_two, *near_all_got = ends(False, [])
            far_one, far_two, *far_all_got = ends(True, [near_one, near_two])
            near_made = middles(False, near_one, near_two, [far_one, far_two])
            far_made = middles(True, far_one, far_two, [near_made[0], far_one, far_two])
        else:
            near_one, near_two, *near_all_got = ends(False, [])
            near_made = middles(False, near_one, near_two, [])
            far_one, far_two, *far_all_got = ends(True, [near_made[0], near_one, near_two])
            far_made = middles(True, far_one, far_two, [])
        after = [far_made[0], far_one, far_two]
        near_ends = (near_one, near_two, near_made[0], *near_all_got, vert_weight[p])
        far_ends = (far_one, far_two, far_made[0], *far_all_got, vert_weight[p])
        near_made, far_made = near_made[1:], far_made[1:]
        if last:
            near_rows = call(last_kernel, edge(slots), [VMEM] * 9, after=after)(counts, ends_now[0], *near_ends, near_made[0])
            return call(
                final_kernel,
                jax.ShapeDtypeStruct(field.shape, BF16),
                [VMEM] * 10,
                [pltpu.VMEM((slots, H, lons, channels), BF16), pltpu.SemaphoreType.DMA((2 * H, slots))],
                out_specs=hbm,
            )(counts, ends_now[1], *far_ends, far_made[0], near_rows)
        middle_far = far_made[1]
        middle_far_got = lax.ppermute(middle_far, "lat", far_pairs)
        maps = maps_of(p + 1, after)
        new_near, near = call(functools.partial(mix_kernel, False), [edge(2), edge(3)], [VMEM] * 10, after=[maps])(
            counts, field, *near_ends, norm_gain, near_made[1]
        )
        near_got = lax.ppermute(near, "lat", near_pairs)
        new_far, far = call(functools.partial(mix_kernel, True), [edge(2), edge(2)], [VMEM] * 10, after=[near], cost=10**10)(
            counts, field, *far_ends, norm_gain, middle_far
        )
        far_got = lax.ppermute(far, "lat", far_pairs)
        ends_edges = (far, near, far_got, near_got)
        middle_edges = (middle_far, near, middle_far_got, near_got)
        middle_at = ((0, 2, 2), (0, 2, 0))
        ends_now, middle_now = (new_near, new_far), (near_made[0], far_made[0])


def solution(mesh):
    return jax.shard_map(
        on_device,
        mesh=mesh,
        in_specs=(P("lev", "lat", None, None), P(), P(), P(), P(), P(), P(), P()),
        out_specs=P("lev", "lat", None, None),
        check_vma=False,
    )
```
